32 devices in a mesh: blk: 16 (over z, y, x), grp: 2 (over core).
Axes of the slice: x: 2, y: 2, z: 4, core: 2. Of those that a mesh axis runs over, the one named last changes fastest.
Arguments:
- excitation: bfloat16 [32, 1024, 256], P('blk'), may hold values from -6 to 6
- inverse_self: bfloat16 [32, 1024, 1024], P('blk', 'grp'), may hold values from -0.1875 to 0.1875
- coupling: bfloat16 [32, 4, 1024, 1024], P('blk', None, 'grp'), may hold values from -0.1875 to 0.1875
- neighbour_mask: int32 [32, 4], P('blk'), may hold values 0 or 1
- sketch: float32 [5, 256, 32], replicated, may hold values from -6 to 6
Outputs:
- bases: float32 [32, 1024, 32], P('blk', 'grp')
- reduced_coupling: float32 [32, 4, 32, 32], P('blk')
- reduced_excitation: float32 [32, 32, 256], P('blk')
The draws below stay inside these ranges and needn't reach their ends.
Inputs may be any that keep to these rules, and one draw needn't show every extreme that they name: `neighbour_mask`: 1 where the block at that slot's offset adds secondary currents, 0 where it does not; slots pointing outside the array add nothing in any case.
All inputs are finite; a program needn't handle non-finite values.
Results may differ from the reference program's by a relative error of at most 0.0003.
Values sent between devices are 32-bit elements; how exact they have to be, the bound alone decides.
A program may use at most 64 MiB of HBM per device.

```python
import math
import jax
import jax.numpy as jnp
from jax import lax

N = 1024
P_SIZE = 256
R = 32
K = 4
NB = 32


def set_ends(entries, rng, least, top_value):
    longest = entries.shape.index(max(entries.shape))
    spots = []
    for shift in (0, 1):
        where = [jax.random.randint(jax.random.fold_in(rng, axis), (), 0, length) for axis, length in enumerate(entries.shape)]
        where[longest] = (where[longest] + shift) % entries.shape[longest]
        spots.append(tuple(where))
    return entries.at[spots[0]].set(least).at[spots[1]].set(top_value)


def level_of(stream_key, dims, pieces, low, high):
    factor_of, own = 1.0, jax.random.fold_in(stream_key, 6)
    for axis_at, shards_of in pieces:
        steps = jnp.exp(jax.random.uniform(jax.random.fold_in(own, axis_at), (shards_of,), jnp.float32, low / len(pieces), high / len(pieces)))
        factor_of = factor_of * jnp.repeat(steps, dims[axis_at] // shards_of).reshape([-1 if axis == axis_at else 1 for axis in range(len(dims))])
    return factor_of


def gaussian(key, extent, width, bound, cuts=(), kind=jnp.bfloat16):
    drawn = width * jax.random.normal(key, extent, jnp.float32)
    if cuts:
        drawn = drawn * level_of(key, extent, cuts, -0.22, 0.18)
    return jnp.clip(drawn, -bound, bound).astype(kind)


def setup_inputs(seed: int = 0) -> dict:
    key_of = jax.random.split(jax.random.key(seed), 6)
    return {
        "excitation": gaussian(key_of[0], (NB, N, P_SIZE), 1.0, 6.0, ((0, 16),)),
        "inverse_self": gaussian(key_of[1], (NB, N, N), N ** -0.5, 0.1875, ((0, 16), (1, 2))),
        "coupling": gaussian(key_of[2], (NB, K, N, N), N ** -0.5, 0.1875, ((0, 16), (2, 2))),
        "neighbour_mask": set_ends((jax.random.randint(key_of[3], (NB, K), 0, 4) < 3).astype(jnp.int32), jax.random.fold_in(key_of[3], 1), 0, 1),
        "sketch": gaussian(key_of[4], (K + 1, P_SIZE, R), 1.0, 6.0, (), jnp.float32),
    }


neighbour_offsets = (-2, -1, 1, 2)

def exact_dot(left, right):
    return jnp.dot(left.astype(jnp.float32), right.astype(jnp.float32), precision=lax.Precision.HIGHEST, preferred_element_type=jnp.float32)

def reference(excitation, inverse_self, coupling, neighbour_mask, sketch):
    primary = lax.map(lambda pair: jnp.dot(pair[0].astype(jnp.float32), pair[1].astype(jnp.float32), preferred_element_type=jnp.float32), (inverse_self, excitation))
    padding = jnp.zeros((2, N, P_SIZE), jnp.float32)
    padded = jnp.concatenate([padding, primary, padding], axis=0)
    weights_mask = neighbour_mask.astype(jnp.float32)

    def sketch_block(index):
        beside_all = lax.dynamic_slice_in_dim(padded, index, 5, 0)
        sources = jnp.zeros((N, R), jnp.float32)
        for slot_index, offset in enumerate(neighbour_offsets):
            coupled = exact_dot(coupling[index, slot_index], beside_all[2 + offset])
            coupled = exact_dot(coupled, sketch[slot_index + 1])
            sources = sources + weights_mask[index, slot_index] * coupled
        own_part = exact_dot(primary[index], sketch[0])
        return own_part - exact_dot(inverse_self[index], sources)
    sketched = lax.map(sketch_block, jnp.arange(NB, dtype=jnp.int32))
    gram = jnp.einsum('bnr,bns->brs', sketched, sketched, precision=lax.Precision.HIGHEST) / N
    chol_lower = jnp.linalg.cholesky(gram)
    bases = lax.linalg.triangular_solve(chol_lower, sketched, left_side=False, lower=True, transpose_a=True)
    base_pad = jnp.zeros((2, N, R), jnp.float32)
    padded_bases = jnp.concatenate([base_pad, bases, base_pad], axis=0)
    norm_scale = 1.0 / math.sqrt(N)

    def reduce_block(index):
        beside_all = lax.dynamic_slice_in_dim(padded_bases, index, 5, 0)
        own_basis = bases[index]
        stacked = []
        for slot_index, offset in enumerate(neighbour_offsets):
            coupled = exact_dot(coupling[index, slot_index], beside_all[2 + offset])
            stacked.append(exact_dot(own_basis.T, coupled))
        driven = exact_dot(own_basis.T, excitation[index])
        return (jnp.stack(stacked, axis=0) * norm_scale, driven * norm_scale)
    reduced_coupling, reduced_excitation = lax.map(reduce_block, jnp.arange(NB, dtype=jnp.int32))
    return (bases, reduced_coupling, reduced_excitation)
```

```python
import functools
import math

import jax
import jax.numpy as jnp
from jax import lax
from jax.experimental import pallas as pl
from jax.experimental.pallas import tpu as pltpu
from jax.sharding import PartitionSpec as P

MESH = pl.DeviceIdType.MESH
F32, BF16 = jnp.float32, jnp.bfloat16

PIECES = (
    (0, 0, 1, 0),
    (0, 2, -1, 3),
    (0, 3, -1, 4),
    (0, 1, 0, 6),
    (1, 1, 1, 2),
    (1, 3, -1, 5),
    (1, 0, 1, 1),
    (1, 2, 0, 7),
)
USE = {0: (0, 0), 1: (1, 0), 2: (0, 1), 3: (1, 2), 4: (0, 3), 5: (1, 3), 6: (1, 1), 7: (0, 2)}


def nt(left, right):
    return lax.dot_general(left, right, (((1,), (1,)), ((), ())), preferred_element_type=F32)


def nn(left, right):
    return lax.dot_general(left, right, (((1,), (0,)), ((), ())), preferred_element_type=F32)


def terms(x, count):
    out = []
    for step in range(count):
        part = x.astype(BF16)
        out.append(part)
        if step < count - 1:
            x = x - part.astype(F32)
    return out


def stacked(x, count):
    return jnp.concatenate(terms(x, count), axis=0)


def folded(x, count):
    size = x.shape[0] // count
    total = x[:size]
    for step in range(1, count):
        total = total + x[step * size : (step + 1) * size]
    return total


def exact_nt(left, right, count):
    rows = left.shape[0]
    ls, rs = terms(left, count), terms(right, count)
    total = None
    for order in range(count):
        got = nt(jnp.concatenate(ls[: count - order], axis=0), rs[order])
        got = folded(got, count - order)
        total = got if total is None else total + got
    return total


def exact_nn(left, right, count):
    ls, rs = terms(left, count), terms(right, count)
    total = None
    for order in range(count):
        got = nn(jnp.concatenate(ls[: count - order], axis=0), rs[order])
        got = folded(got, count - order)
        total = got if total is None else total + got
    return total


def inverse_factors(grams):
    size = grams[0].shape[0]
    row = lax.broadcasted_iota(jnp.int32, (size, size), 0)
    col = lax.broadcasted_iota(jnp.int32, (size, size), 1)
    eye = (row == col).astype(F32)
    down = lax.broadcasted_iota(jnp.int32, (size, 1), 0)
    work = [jnp.concatenate([gram, eye], axis=1) for gram in grams]
    for k in range(size - 1):
        for n, a in enumerate(work):
            line = a[k : k + 1, :] / a[k : k + 1, k : k + 1]
            lead = jnp.where(down > k, a[:, k : k + 1], 0.0)
            work[n] = a - lead * line
    out = []
    for a in work:
        diag = jnp.sum(jnp.where(row == col, a[:, :size], 0.0), axis=1, keepdims=True)
        out.append(a[:, size:] / jnp.sqrt(diag))
    return out


def kernel(
    g_size, b_size, ex, inv, coup, mask, sketch, bases_o, rc_o, re_o,
    ex_v, inv_v, c_v, sk_v, out_v, buf, src, skt, near, lin, lin_near, wbuf, y_v, bases_v, rc_v, re_v,
    load_sem, store_sem, p1_send, p1_recv, p1_fsend, p1_frecv, src_send, src_recv,
    sk_send, sk_recv, skp_send, skp_recv, skf_send, skf_recv, lin_send, lin_recv, w_send, w_recv,
):
    b, g = lax.axis_index("blk"), lax.axis_index("grp")
    has_left, has_right = b > 0, b < b_size - 1
    blocks, unknowns, _ = ex.shape
    rows = inv.shape[1]
    slots = coup.shape[1]
    r = sketch.shape[2]
    peers = [lax.rem(g + d, g_size) for d in range(1, g_size)]

    def load(number, source, target):
        return pltpu.make_async_copy(source, target, load_sem.at[number])

    loads = {}
    loads["sketch"] = load(0, sketch, sk_v)
    for i in range(blocks):
        loads["inv", i] = load(1 + 2 * i, inv.at[i], inv_v.at[i])
        loads["ex", i] = load(2 + 2 * i, ex.at[i], ex_v.at[i])
    for number, place in enumerate((6, 7, 0, 3, 4, 2, 5, 1)):
        i, k = USE[place]
        loads["c", i, k] = load(1 + 2 * blocks + number, coup.at[i, k], c_v.at[i, k])
    for copy in loads.values():
        copy.start()

    barrier = pltpu.get_barrier_semaphore()

    @pl.when(has_left)
    def _():
        pl.semaphore_signal(barrier, inc=1, device_id=(b - 1, g), device_id_type=MESH)

    @pl.when(has_right)
    def _():
        pl.semaphore_signal(barrier, inc=1, device_id=(b + 1, g), device_id_type=MESH)

    for peer in peers:
        pl.semaphore_signal(barrier, inc=1, device_id=(b, peer), device_id_type=MESH)
    pl.semaphore_wait(barrier, g_size - 1 + has_left.astype(jnp.int32) + has_right.astype(jnp.int32))

    def remote(source, target, send, recv, device):
        return pltpu.make_async_remote_copy(
            src_ref=source, dst_ref=target, send_sem=send, recv_sem=recv,
            device_id=device, device_id_type=MESH,
        )

    def to_peers(source, target, send, recv):
        return [
            remote(source, target, send.at[d], recv.at[d], (b, peer)) for d, peer in enumerate(peers)
        ]

    def there(direction):
        return has_left if direction > 0 else has_right

    def sends(direction):
        return has_right if direction > 0 else has_left

    @pl.when(jnp.logical_not(has_left))
    def _():
        for p in range(g_size):
            buf[p, 0 : 3 * r, :] = jnp.zeros((3 * r, rows), F32)
            near[0, p] = jnp.zeros((2 * r, rows), F32)
        lin_near[0] = jnp.zeros(lin_near.shape[1:], F32)

    @pl.when(jnp.logical_not(has_right))
    def _():
        for p in range(g_size):
            buf[p, 3 * r : 6 * r, :] = jnp.zeros((3 * r, rows), F32)
            near[1, p] = jnp.zeros((2 * r, rows), F32)
        lin_near[1] = jnp.zeros(lin_near.shape[1:], F32)

    loads["sketch"].wait()
    order = list(range(1, slots + 1)) + [0]
    flat = jnp.concatenate([sk_v[k].T for k in order], axis=0)
    flat_hi, flat_lo = terms(flat, 2)
    flat_both = jnp.concatenate([flat_hi, flat_lo], axis=0)

    piece_copies, own_copies = {}, {}
    for i in range(blocks):
        loads["inv", i].wait()
        loads["ex", i].wait()
        primary = nn(inv_v[i], ex_v[i])
        primary_hi, primary_lo = terms(primary, 2)
        got = folded(nt(flat_both, primary_hi), 2) + nt(flat_hi, primary_lo)
        out_v[i] = got
        for number, (block, slot, direction, place) in enumerate(PIECES):
            if block != i:
                continue
            here = buf.at[g, pl.ds(place * r, r)]
            if direction == 0:
                buf[g, pl.ds(place * r, r), :] = got[slot * r : (slot + 1) * r]
                own_copies[place] = to_peers(here, here, p1_fsend.at[place], p1_frecv.at[place])
                for copy in own_copies[place]:
                    copy.start()
            else:
                copy = remote(
                    out_v.at[i, pl.ds(slot * r, r)], here, p1_send.at[place], p1_recv.at[place],
                    (b + direction, g),
                )
                piece_copies[place] = (direction, copy)
                pl.when(sends(direction))(copy.start)

    def coupled(i, k, parts):
        total = None
        for p in range(g_size):
            got = nt(stacked(parts[p], 3), c_v[i, k, :, p * rows : (p + 1) * rows])
            total = got if total is None else total + got
        return folded(total, 3)

    weights = [[mask[i, k].astype(F32) for k in range(slots)] for i in range(blocks)]
    sources = [None] * blocks

    def add_source(place):
        i, k = USE[place]
        loads["c", i, k].wait()
        term = weights[i][k] * coupled(i, k, [buf[p, place * r : (place + 1) * r, :] for p in range(g_size)])
        sources[i] = term if sources[i] is None else sources[i] + term

    def forward(places):
        for place in places:
            direction, copy = piece_copies[place]
            here = buf.at[g, pl.ds(place * r, r)]
            own_copies[place] = to_peers(here, here, p1_fsend.at[place], p1_frecv.at[place])

            @pl.when(there(direction))
            def _():
                copy.wait_recv()
                for out in own_copies[place]:
                    out.start()

    def arrived(place):
        if place in piece_copies:

            @pl.when(there(piece_copies[place][0]))
            def _():
                for out in own_copies[place]:
                    out.wait_recv()
        else:
            for out in own_copies[place]:
                out.wait_recv()

    src_copies, sk_copies, skp_copies = {}, {}, {}

    def finish_source(i):
        src[g, i * r : (i + 1) * r, :] = sources[i]
        here = src.at[g, pl.ds(i * r, r)]
        src_copies[i] = to_peers(here, here, src_send.at[i], src_recv.at[i])
        for copy in src_copies[i]:
            copy.start()

    for place in (6, 7):
        arrived(place)
        add_source(place)
    forward((0, 3, 4))
    arrived(0)
    add_source(0)
    forward((2, 5))
    arrived(3)
    add_source(3)
    arrived(4)
    add_source(4)
    forward((1,))
    arrived(2)
    add_source(2)
    finish_source(0)
    arrived(5)
    add_source(5)
    arrived(1)
    add_source(1)
    finish_source(1)

    for i in range(blocks):
        for copy in src_copies[i]:
            copy.wait_recv()
        total = None
        for p in range(g_size):
            got = nt(
                stacked(src[p, i * r : (i + 1) * r, :], 3), inv_v[i, :, p * rows : (p + 1) * rows]
            )
            total = got if total is None else total + got
        skt[g, i * r : (i + 1) * r, :] = out_v[i, slots * r : (slots + 1) * r, :] - folded(total, 3)
        here = skt.at[g, pl.ds(i * r, r)]
        for side, direction in enumerate((1, -1)):
            copy = remote(
                here, near.at[side, g, pl.ds(i * r, r)], sk_send.at[side, i], sk_recv.at[side, i],
                (b + direction, g),
            )
            sk_copies[side, i] = (direction, copy)
            pl.when(sends(direction))(copy.start)
        skp_copies[i] = to_peers(here, here, skp_send.at[i], skp_recv.at[i])
        for copy in skp_copies[i]:
            copy.start()

    grams = []
    for i in range(blocks):
        for copy in skp_copies[i]:
            copy.wait_recv()
        total = None
        for p in range(g_size):
            part = skt[p, i * r : (i + 1) * r, :]
            got = exact_nt(part, part, 3)
            total = got if total is None else total + got
        grams.append(total * (1.0 / unknowns))
    inverses = inverse_factors(grams)
    for i in range(blocks):
        lin[i * r : (i + 1) * r, :] = jnp.concatenate([inverses[i]] * slots, axis=1)
    lin_copies = []
    for side, direction in enumerate((1, -1)):
        copy = remote(lin, lin_near.at[side], lin_send.at[side], lin_recv.at[side], (b + direction, g))
        lin_copies.append((direction, copy))
        pl.when(sends(direction))(copy.start)

    skf_copies = {}

    def forward_sketched(side, i):
        direction, copy = sk_copies[side, i]
        here = near.at[side, g, pl.ds(i * r, r)]
        skf_copies[side, i] = to_peers(here, here, skf_send.at[side, i], skf_recv.at[side, i])

        @pl.when(there(direction))
        def _():
            copy.wait_recv()
            for out in skf_copies[side, i]:
                out.start()

    def arrived_sketched(side, i):
        @pl.when(there(sk_copies[side, i][0]))
        def _():
            for out in skf_copies[side, i]:
                out.wait_recv()

    for side in range(2):
        forward_sketched(side, 0)

    scale = 1.0 / math.sqrt(unknowns)
    bases_t = []
    for i in range(blocks):
        own = exact_nn(inverses[i], skt[g, i * r : (i + 1) * r, :], 3)
        bases_t.append(own)
        bases_v[i] = own.T
        driven = None
        for p in range(g_size):
            got = nn(stacked(skt[p, i * r : (i + 1) * r, :], 3), ex_v[i, p * rows : (p + 1) * rows, :])
            driven = got if driven is None else driven + got
        re_v[i] = exact_nn(inverses[i], folded(driven, 3), 3) * scale
    stores = [
        pltpu.make_async_copy(bases_v, bases_o, store_sem.at[0]),
        pltpu.make_async_copy(re_v, re_o, store_sem.at[1]),
    ]
    for copy in stores:
        copy.start()

    def couple_basis(i, k, parts):
        y_v[i, k * r : (k + 1) * r, :] = coupled(i, k, parts)

    couple_basis(0, 2, [skt[p, r : 2 * r, :] for p in range(g_size)])
    for side in range(2):
        forward_sketched(side, 1)
    couple_basis(1, 1, [skt[p, 0:r, :] for p in range(g_size)])

    arrived_sketched(0, 0)
    couple_basis(0, 0, [near[0, p, 0:r, :] for p in range(g_size)])
    arrived_sketched(1, 0)
    parts = [near[1, p, 0:r, :] for p in range(g_size)]
    couple_basis(0, 3, parts)
    couple_basis(1, 2, parts)
    arrived_sketched(0, 1)
    parts = [near[0, p, r : 2 * r, :] for p in range(g_size)]
    couple_basis(0, 1, parts)
    couple_basis(1, 0, parts)
    arrived_sketched(1, 1)
    couple_basis(1, 3, [near[1, p, r : 2 * r, :] for p in range(g_size)])

    for direction, copy in lin_copies:
        pl.when(there(direction))(copy.wait_recv)

    wide = slots * r
    row = lax.broadcasted_iota(jnp.int32, (wide, wide), 0) // r
    col = lax.broadcasted_iota(jnp.int32, (wide, wide), 1) // r
    left_a, left_b = lin_near[0, 0:r, :], lin_near[0, r : 2 * r, :]
    right_a, right_b = lin_near[1, 0:r, :], lin_near[1, r : 2 * r, :]
    own_a, own_b = lin[0:r, :], lin[r : 2 * r, :]
    beside = ((left_a, left_b, own_b, right_a), (left_b, own_a, right_a, right_b))
    for i in range(blocks):
        product = exact_nt(bases_t[i], y_v[i], 3)
        factors = jnp.where(row == col, jnp.concatenate(beside[i], axis=0), 0.0)
        wbuf[g, i * r : (i + 1) * r, :] = exact_nt(product, factors, 3)
    here = wbuf.at[g]
    w_copies = to_peers(here, here, w_send, w_recv)
    for copy in w_copies:
        copy.start()
    for copy in w_copies:
        copy.wait_recv()
    total = wbuf[0]
    for p in range(1, g_size):
        total = total + wbuf[p]
    total = total * scale
    for i in range(blocks):
        for k in range(slots):
            rc_v[i, k] = total[i * r : (i + 1) * r, k * r : (k + 1) * r]
    last = pltpu.make_async_copy(rc_v, rc_o, store_sem.at[2])
    last.start()

    for direction, copy in list(piece_copies.values()) + list(sk_copies.values()) + lin_copies:
        pl.when(sends(direction))(copy.wait_send)
    for place, copies in own_copies.items():
        for copy in copies:
            if place in piece_copies:
                pl.when(there(piece_copies[place][0]))(copy.wait_send)
            else:
                copy.wait_send()
    for (side, i), copies in skf_copies.items():
        for copy in copies:
            pl.when(there(sk_copies[side, i][0]))(copy.wait_send)
    for copies in list(src_copies.values()) + list(skp_copies.values()) + [w_copies]:
        for copy in copies:
            copy.wait_send()
    for copy in stores:
        copy.wait()
    last.wait()


def shards(g_size, b_size, excitation, inverse_self, coupling, neighbour_mask, sketch):
    blocks, unknowns, columns = excitation.shape
    rows = inverse_self.shape[1]
    slots = coupling.shape[1]
    r = sketch.shape[2]
    assert blocks == 2 and slots == 4 and rows * g_size == unknowns
    others = max(g_size - 1, 1)
    wide = slots * r
    vmem = lambda *shape: pltpu.VMEM(shape, F32)
    dma = lambda *shape: pltpu.SemaphoreType.DMA(shape)
    anywhere = pl.BlockSpec(memory_space=pl.ANY)
    flops = 2 * blocks * rows * unknowns * (columns + 2 * slots * 3 * r)
    return pl.pallas_call(
        functools.partial(kernel, g_size, b_size),
        out_shape=(
            jax.ShapeDtypeStruct((blocks, rows, r), F32),
            jax.ShapeDtypeStruct((blocks, slots, r, r), F32),
            jax.ShapeDtypeStruct((blocks, r, columns), F32),
        ),
        in_specs=[anywhere, anywhere, anywhere, pl.BlockSpec(memory_space=pltpu.SMEM), anywhere],
        out_specs=(anywhere, anywhere, anywhere),
        scratch_shapes=[
            pltpu.VMEM(excitation.shape, BF16),
            pltpu.VMEM(inverse_self.shape, BF16),
            pltpu.VMEM(coupling.shape, BF16),
            vmem(*sketch.shape),
            vmem(blocks, (slots + 1) * r, rows),
            vmem(g_size, 8 * r, rows),
            vmem(g_size, 2 * r, rows),
            vmem(g_size, 2 * r, rows),
            vmem(2, g_size, 2 * r, rows),
            vmem(2 * r, wide),
            vmem(2, 2 * r, wide),
            vmem(g_size, 2 * r, wide),
            vmem(blocks, wide, rows),
            vmem(blocks, rows, r),
            vmem(blocks, slots, r, r),
            vmem(blocks, r, columns),
            dma(1 + 2 * blocks + blocks * slots),
            dma(3),
            dma(6),
            dma(6),
            dma(8, others),
            dma(8, others),
            dma(blocks, others),
            dma(blocks, others),
            dma(2, blocks),
            dma(2, blocks),
            dma(blocks, others),
            dma(blocks, others),
            dma(2, blocks, others),
            dma(2, blocks, others),
            dma(2),
            dma(2),
            dma(others),
            dma(others),
        ],
        compiler_params=pltpu.CompilerParams(
            collective_id=0, has_side_effects=True, vmem_limit_bytes=48 * 1024 * 1024
        ),
        cost_estimate=pl.CostEstimate(
            flops=flops, bytes_accessed=2 * (coupling.size + inverse_self.size), transcendentals=0
        ),
        name="basis_currents",
    )(excitation, inverse_self, coupling, neighbour_mask, sketch)


def solution(mesh):
    return jax.shard_map(
        functools.partial(shards, mesh.shape["grp"], mesh.shape["blk"]),
        mesh=mesh,
        in_specs=(
            P("blk", None, None),
            P("blk", "grp", None),
            P("blk", None, "grp", None),
            P("blk", None),
            P(),
        ),
        out_specs=(P("blk", "grp", None), P("blk", None, None, None), P("blk", None, None)),
        check_vma=False,
    )
```

```python
import functools
import math

import jax
import jax.numpy as jnp
from jax import lax
from jax.experimental import pallas as pl
from jax.experimental.pallas import tpu as pltpu
from jax.sharding import PartitionSpec as P

MESH = pl.DeviceIdType.MESH
F32, BF16 = jnp.float32, jnp.bfloat16

PIECES = (
    (0, 0, 1, 0),
    (0, 3, -1, 4),
    (0, 1, 0, 6),
    (1, 1, 1, 2),
    (1, 2, 0, 7),
    (0, 2, -1, 3),
    (1, 0, 1, 1),
    (1, 3, -1, 5),
)
USE = {0: (0, 0), 1: (1, 0), 2: (0, 1), 3: (1, 2), 4: (0, 3), 5: (1, 3), 6: (1, 1), 7: (0, 2)}


def nt(left, right):
    return lax.dot_general(left, right, (((1,), (1,)), ((), ())), preferred_element_type=F32)


def nn(left, right):
    return lax.dot_general(left, right, (((1,), (0,)), ((), ())), preferred_element_type=F32)


def terms(x, count):
    out = []
    for step in range(count):
        part = x.astype(BF16)
        out.append(part)
        if step < count - 1:
            x = x - part.astype(F32)
    return out


def stacked(x, count):
    return jnp.concatenate(terms(x, count), axis=0)


def folded(x, count):
    size = x.shape[0] // count
    total = x[:size]
    for step in range(1, count):
        total = total + x[step * size : (step + 1) * size]
    return total


def exact_nt(left, right, count):
    rows = left.shape[0]
    ls, rs = terms(left, count), terms(right, count)
    total = None
    for order in range(count):
        got = nt(jnp.concatenate(ls[: count - order], axis=0), rs[order])
        got = folded(got, count - order)
        total = got if total is None else total + got
    return total


def exact_nn(left, right, count):
    ls, rs = terms(left, count), terms(right, count)
    total = None
    for order in range(count):
        got = nn(jnp.concatenate(ls[: count - order], axis=0), rs[order])
        got = folded(got, count - order)
        total = got if total is None else total + got
    return total


def inverse_factors(grams):
    size = grams[0].shape[0]
    row = lax.broadcasted_iota(jnp.int32, (size, size), 0)
    col = lax.broadcasted_iota(jnp.int32, (size, size), 1)
    eye = (row == col).astype(F32)
    down = lax.broadcasted_iota(jnp.int32, (size, 1), 0)
    work = [jnp.concatenate([gram, eye], axis=1) for gram in grams]
    for k in range(size - 1):
        for n, a in enumerate(work):
            line = a[k : k + 1, :] / a[k : k + 1, k : k + 1]
            lead = jnp.where(down > k, a[:, k : k + 1], 0.0)
            work[n] = a - lead * line
    out = []
    for a in work:
        diag = jnp.sum(jnp.where(row == col, a[:, :size], 0.0), axis=1, keepdims=True)
        out.append(a[:, size:] / jnp.sqrt(diag))
    return out


def kernel(
    g_size, b_size, ex, inv, coup, mask, sketch, bases_o, rc_o, re_o,
    ex_v, inv_v, c_v, sk_v, out_v, buf, src, skt, near, lin, lin_near, wbuf, v_out, v_in, bases_v, rc_v, re_v,
    load_sem, store_sem, p1_send, p1_recv, p1_fsend, p1_frecv, src_send, src_recv,
    sk_send, sk_recv, skp_send, skp_recv, v_send, v_recv, lin_send, lin_recv, w_send, w_recv,
):
    b, g = lax.axis_index("blk"), lax.axis_index("grp")
    has_left, has_right = b > 0, b < b_size - 1
    blocks, unknowns, _ = ex.shape
    rows = inv.shape[1]
    slots = coup.shape[1]
    r = sketch.shape[1]
    peers = [lax.rem(g + d, g_size) for d in range(1, g_size)]

    def load(number, source, target):
        return pltpu.make_async_copy(source, target, load_sem.at[number])

    loads = {}
    loads["sketch"] = load(0, sketch, sk_v)
    for i in range(blocks):
        loads["inv", i] = load(1 + 2 * i, inv.at[i], inv_v.at[i])
        loads["ex", i] = load(2 + 2 * i, ex.at[i], ex_v.at[i])
    for number, place in enumerate((7, 6, 0, 4, 2, 3, 1, 5)):
        i, k = USE[place]
        loads["c", i, k] = load(1 + 2 * blocks + number, coup.at[i, k], c_v.at[i, k])
    for copy in loads.values():
        copy.start()

    barrier = pltpu.get_barrier_semaphore()

    @pl.when(has_left)
    def _():
        pl.semaphore_signal(barrier, inc=1, device_id=(b - 1, g), device_id_type=MESH)

    @pl.when(has_right)
    def _():
        pl.semaphore_signal(barrier, inc=1, device_id=(b + 1, g), device_id_type=MESH)

    for peer in peers:
        pl.semaphore_signal(barrier, inc=1, device_id=(b, peer), device_id_type=MESH)

    def remote(source, target, send, recv, device):
        return pltpu.make_async_remote_copy(
            src_ref=source, dst_ref=target, send_sem=send, recv_sem=recv,
            device_id=device, device_id_type=MESH,
        )

    def to_peers(source, target, send, recv):
        return [
            remote(source, target, send.at[d], recv.at[d], (b, peer)) for d, peer in enumerate(peers)
        ]

    def there(direction):
        return has_left if direction > 0 else has_right

    def sends(direction):
        return has_right if direction > 0 else has_left

    @pl.when(jnp.logical_not(has_left))
    def _():
        for p in range(g_size):
            buf[p, 0 : 3 * r, :] = jnp.zeros((3 * r, rows), F32)
        near[0] = jnp.zeros(near.shape[1:], F32)
        lin_near[0] = jnp.zeros(lin_near.shape[1:], F32)

    @pl.when(jnp.logical_not(has_right))
    def _():
        for p in range(g_size):
            buf[p, 3 * r : 6 * r, :] = jnp.zeros((3 * r, rows), F32)
        near[1] = jnp.zeros(near.shape[1:], F32)
        lin_near[1] = jnp.zeros(lin_near.shape[1:], F32)

    loads["sketch"].wait()
    order = list(range(1, slots + 1)) + [0]
    flat = jnp.concatenate([sk_v[k] for k in order], axis=0)
    flat_hi, flat_lo = terms(flat, 2)
    flat_both = jnp.concatenate([flat_hi, flat_lo], axis=0)

    piece_copies, own_copies = {}, {}

    def send_piece(block, slot, direction, place):
        here = buf.at[g, pl.ds(place * r, r)]
        if direction == 0:
            buf[g, pl.ds(place * r, r), :] = out_v[block, slot * r : (slot + 1) * r, :]
            own_copies[place] = to_peers(here, here, p1_fsend.at[place], p1_frecv.at[place])
            for copy in own_copies[place]:
                copy.start()
        else:
            copy = remote(
                out_v.at[block, pl.ds(slot * r, r)], here, p1_send.at[place], p1_recv.at[place],
                (b + direction, g),
            )
            piece_copies[place] = (direction, copy)
            pl.when(sends(direction))(copy.start)

    for i in range(blocks):
        loads["inv", i].wait()
        loads["ex", i].wait()
        primary = nn(inv_v[i], ex_v[i])
        primary_hi, primary_lo = terms(primary, 2)
        out_v[i] = folded(nt(flat_both, primary_hi), 2) + nt(flat_hi, primary_lo)
        if i == 0:
            neighbours = has_left.astype(jnp.int32) + has_right.astype(jnp.int32)
            pl.semaphore_wait(barrier, g_size - 1 + neighbours)
        for piece in PIECES[:3] if i == 0 else PIECES[3:]:
            send_piece(*piece)

    def coupled(i, k, parts):
        total = None
        for p in range(g_size):
            got = nt(stacked(parts[p], 3), c_v[i, k, :, p * rows : (p + 1) * rows])
            total = got if total is None else total + got
        return folded(total, 3)

    weights = [[mask[i, k].astype(F32) for k in range(slots)] for i in range(blocks)]
    sources = [None] * blocks

    def add_source(place):
        i, k = USE[place]
        loads["c", i, k].wait()
        term = weights[i][k] * coupled(i, k, [buf[p, place * r : (place + 1) * r, :] for p in range(g_size)])
        sources[i] = term if sources[i] is None else sources[i] + term

    def forward(places):
        for place in places:
            direction, copy = piece_copies[place]
            here = buf.at[g, pl.ds(place * r, r)]
            own_copies[place] = to_peers(here, here, p1_fsend.at[place], p1_frecv.at[place])

            @pl.when(there(direction))
            def _():
                copy.wait_recv()
                for out in own_copies[place]:
                    out.start()

    def arrived(place):
        if place in piece_copies:

            @pl.when(there(piece_copies[place][0]))
            def _():
                for out in own_copies[place]:
                    out.wait_recv()
        else:
            for out in own_copies[place]:
                out.wait_recv()

    src_copies, sk_copies, skp_copies, v_copies = {}, {}, {}, {}

    def finish_source(i):
        src[g, i * r : (i + 1) * r, :] = sources[i]
        here = src.at[g, pl.ds(i * r, r)]
        src_copies[i] = to_peers(here, here, src_send.at[i], src_recv.at[i])
        for copy in src_copies[i]:
            copy.start()

    def sketch_block(i):
        for copy in src_copies[i]:
            copy.wait_recv()
        total = None
        for p in range(g_size):
            got = nt(
                stacked(src[p, i * r : (i + 1) * r, :], 3), inv_v[i, :, p * rows : (p + 1) * rows]
            )
            total = got if total is None else total + got
        skt[g, i * r : (i + 1) * r, :] = out_v[i, slots * r : (slots + 1) * r, :] - folded(total, 3)
        here = skt.at[g, pl.ds(i * r, r)]
        for side, direction in enumerate((1, -1)):
            copy = remote(
                here, near.at[side, pl.ds(i * r, r)], sk_send.at[side, i], sk_recv.at[side, i],
                (b + direction, g),
            )
            sk_copies[side, i] = (direction, copy)
            pl.when(sends(direction))(copy.start)
        skp_copies[i] = to_peers(here, here, skp_send.at[i], skp_recv.at[i])
        for copy in skp_copies[i]:
            copy.start()

    def project(i, k):
        got = folded(nn(stacked(skt[g, i * r : (i + 1) * r, :], 3), c_v[i, k]), 3)
        for p in range(g_size):
            v_out[p, (i * slots + k) * r : (i * slots + k + 1) * r, :] = got[:, p * rows : (p + 1) * rows]

    def send_projected(i):
        span = pl.ds(i * slots * r, slots * r)
        v_copies[i] = [
            remote(
                v_out.at[peer, span], v_in.at[d, span], v_send.at[i, d], v_recv.at[i, d], (b, peer)
            )
            for d, peer in enumerate(peers)
        ]
        for copy in v_copies[i]:
            copy.start()

    for place in (7, 6):
        arrived(place)
        add_source(place)
    forward((0, 4))
    arrived(0)
    add_source(0)
    forward((2,))
    arrived(4)
    add_source(4)
    arrived(2)
    add_source(2)
    finish_source(0)
    forward((3,))
    sketch_block(0)
    forward((1, 5))
    arrived(3)
    add_source(3)
    arrived(1)
    add_source(1)
    arrived(5)
    add_source(5)
    finish_source(1)
    for k in range(slots):
        project(0, k)
    send_projected(0)
    sketch_block(1)
    for k in range(2):
        project(1, k)

    for i in range(blocks):
        for copy in skp_copies[i]:
            copy.wait_recv()
    grams = []
    for i in range(blocks):
        total = None
        for p in range(g_size):
            part = skt[p, i * r : (i + 1) * r, :]
            got = exact_nt(part, part, 3)
            total = got if total is None else total + got
        grams.append(total * (1.0 / unknowns))
    for k in range(2, slots):
        project(1, k)
    send_projected(1)
    inverses = inverse_factors(grams)
    for i in range(blocks):
        lin[i * r : (i + 1) * r, :] = jnp.concatenate([inverses[i]] * slots, axis=1)
    lin_copies = []
    for side, direction in enumerate((1, -1)):
        copy = remote(lin, lin_near.at[side], lin_send.at[side], lin_recv.at[side], (b + direction, g))
        lin_copies.append((direction, copy))
        pl.when(sends(direction))(copy.start)

    scale = 1.0 / math.sqrt(unknowns)
    for i in range(blocks):
        bases_v[i] = exact_nn(inverses[i], skt[g, i * r : (i + 1) * r, :], 3)
        driven = None
        for p in range(g_size):
            got = nn(stacked(skt[p, i * r : (i + 1) * r, :], 3), ex_v[i, p * rows : (p + 1) * rows, :])
            driven = got if driven is None else driven + got
        re_v[i] = exact_nn(inverses[i], folded(driven, 3), 3) * scale
    stores = [
        pltpu.make_async_copy(bases_v, bases_o, store_sem.at[0]),
        pltpu.make_async_copy(re_v, re_o, store_sem.at[1]),
    ]
    for copy in stores:
        copy.start()

    wide = slots * r
    row = lax.broadcasted_iota(jnp.int32, (wide, wide), 0) // r
    col = lax.broadcasted_iota(jnp.int32, (wide, wide), 1) // r
    diagonal = row == col
    projected = []
    for i in range(blocks):
        for copy in v_copies[i]:
            copy.wait_recv()
        span = slice(i * wide, (i + 1) * wide)
        total = v_out[g, pl.ds(i * wide, wide), :]
        for d in range(g_size - 1):
            total = total + v_in[d, span, :]
        factors = jnp.where(diagonal, jnp.concatenate([lin[i * r : (i + 1) * r, :]] * slots, axis=0), 0.0)
        projected.append(exact_nn(factors, total, 3))

    products = {}

    def reduce(users, basis):
        left = [projected[i][k * r : (k + 1) * r] for i, k in users]
        got = exact_nt(left[0] if len(left) == 1 else jnp.concatenate(left, axis=0), basis, 3)
        for n, user in enumerate(users):
            products[user] = got[n * r : (n + 1) * r]

    reduce([(1, 1)], skt[g, 0:r, :])
    reduce([(0, 2)], skt[g, r : 2 * r, :])
    for i, side, users in (
        (0, 0, [(0, 0)]),
        (0, 1, [(0, 3), (1, 2)]),
        (1, 0, [(0, 1), (1, 0)]),
        (1, 1, [(1, 3)]),
    ):
        direction, copy = sk_copies[side, i]
        pl.when(there(direction))(copy.wait_recv)
        reduce(users, near[side, i * r : (i + 1) * r, :])
    for direction, copy in lin_copies:
        pl.when(there(direction))(copy.wait_recv)

    left_a, left_b = lin_near[0, 0:r, :], lin_near[0, r : 2 * r, :]
    right_a, right_b = lin_near[1, 0:r, :], lin_near[1, r : 2 * r, :]
    own_a, own_b = lin[0:r, :], lin[r : 2 * r, :]
    beside = ((left_a, left_b, own_b, right_a), (left_b, own_a, right_a, right_b))
    for i in range(blocks):
        product = jnp.concatenate([products[i, k] for k in range(slots)], axis=1)
        factors = jnp.where(diagonal, jnp.concatenate(beside[i], axis=0), 0.0)
        wbuf[g, i * r : (i + 1) * r, :] = exact_nt(product, factors, 3)
    here = wbuf.at[g]
    w_copies = to_peers(here, here, w_send, w_recv)
    for copy in w_copies:
        copy.start()
    for copy in w_copies:
        copy.wait_recv()
    total = wbuf[0]
    for p in range(1, g_size):
        total = total + wbuf[p]
    total = total * scale
    for i in range(blocks):
        for k in range(slots):
            rc_v[i, k] = total[i * r : (i + 1) * r, k * r : (k + 1) * r]
    last = pltpu.make_async_copy(rc_v, rc_o, store_sem.at[2])
    last.start()

    for direction, copy in list(piece_copies.values()) + list(sk_copies.values()) + lin_copies:
        pl.when(sends(direction))(copy.wait_send)
    for place, copies in own_copies.items():
        for copy in copies:
            if place in piece_copies:
                pl.when(there(piece_copies[place][0]))(copy.wait_send)
            else:
                copy.wait_send()
    for copies in list(src_copies.values()) + list(skp_copies.values()) + list(v_copies.values()) + [w_copies]:
        for copy in copies:
            copy.wait_send()
    for copy in stores:
        copy.wait()
    last.wait()


def hand_over(a, b, c, a_out, b_out, c_out, sems):
    copies = [
        pltpu.make_async_copy(source, target, sems.at[n])
        for n, (source, target) in enumerate(((a, a_out), (b, b_out), (c, c_out)))
    ]
    for copy in copies:
        copy.start()
    for copy in copies:
        copy.wait()


def shards(g_size, b_size, excitation, inverse_self, coupling, neighbour_mask, sketch):
    blocks, unknowns, columns = excitation.shape
    rows = inverse_self.shape[1]
    slots = coupling.shape[1]
    sketch = jnp.swapaxes(sketch, 1, 2)
    r = sketch.shape[1]
    assert blocks == 2 and slots == 4 and rows * g_size == unknowns
    others = max(g_size - 1, 1)
    wide = slots * r
    vmem = lambda *shape: pltpu.VMEM(shape, F32)
    dma = lambda *shape: pltpu.SemaphoreType.DMA(shape)
    anywhere = pl.BlockSpec(memory_space=pl.ANY)
    flops = 2 * blocks * rows * unknowns * (columns + 2 * slots * 3 * r)
    bases, reduced, driven = pl.pallas_call(
        functools.partial(kernel, g_size, b_size),
        out_shape=(
            jax.ShapeDtypeStruct((blocks, r, rows), F32),
            jax.ShapeDtypeStruct((blocks, slots, r, r), F32),
            jax.ShapeDtypeStruct((blocks, r, columns), F32),
        ),
        in_specs=[anywhere, anywhere, anywhere, pl.BlockSpec(memory_space=pltpu.SMEM), anywhere],
        out_specs=(anywhere, anywhere, anywhere),
        scratch_shapes=[
            pltpu.VMEM(excitation.shape, BF16),
            pltpu.VMEM(inverse_self.shape, BF16),
            pltpu.VMEM(coupling.shape, BF16),
            vmem(*sketch.shape),
            vmem(blocks, (slots + 1) * r, rows),
            vmem(g_size, 8 * r, rows),
            vmem(g_size, 2 * r, rows),
            vmem(g_size, 2 * r, rows),
            vmem(2, 2 * r, rows),
            vmem(2 * r, wide),
            vmem(2, 2 * r, wide),
            vmem(g_size, 2 * r, wide),
            vmem(g_size, blocks * wide, rows),
            vmem(others, blocks * wide, rows),
            vmem(blocks, r, rows),
            vmem(blocks, slots, r, r),
            vmem(blocks, r, columns),
            dma(1 + 2 * blocks + blocks * slots),
            dma(3),
            dma(6),
            dma(6),
            dma(8, others),
            dma(8, others),
            dma(blocks, others),
            dma(blocks, others),
            dma(2, blocks),
            dma(2, blocks),
            dma(blocks, others),
            dma(blocks, others),
            dma(blocks, others),
            dma(blocks, others),
            dma(2),
            dma(2),
            dma(others),
            dma(others),
        ],
        compiler_params=pltpu.CompilerParams(
            collective_id=0, has_side_effects=True, vmem_limit_bytes=60 * 1024 * 1024
        ),
        cost_estimate=pl.CostEstimate(
            flops=flops, bytes_accessed=2 * (coupling.size + inverse_self.size), transcendentals=0
        ),
        name="basis_currents",
    )(excitation, inverse_self, coupling, neighbour_mask, sketch)
    results = (bases, reduced, driven)
    bases, reduced, driven = pl.pallas_call(
        hand_over,
        out_shape=tuple(jax.ShapeDtypeStruct(x.shape, x.dtype) for x in results),
        in_specs=[anywhere] * 3,
        out_specs=(anywhere,) * 3,
        scratch_shapes=[dma(3)],
        compiler_params=pltpu.CompilerParams(vmem_limit_bytes=60 * 1024 * 1024),
        name="hand_over",
    )(*results)
    return jnp.swapaxes(bases, 1, 2), reduced, driven


def solution(mesh):
    return jax.shard_map(
        functools.partial(shards, mesh.shape["grp"], mesh.shape["blk"]),
        mesh=mesh,
        in_specs=(
            P("blk", None, None),
            P("blk", "grp", None),
            P("blk", None, "grp", None),
            P("blk", None),
            P(),
        ),
        out_specs=(P("blk", "grp", None), P("blk", None, None, None), P("blk", None, None)),
        check_vma=False,
    )
```

```python
import functools
import math

import jax
import jax.numpy as jnp
from jax import lax
from jax.experimental import pallas as pl
from jax.experimental.pallas import tpu as pltpu
from jax.sharding import PartitionSpec as P

MESH = pl.DeviceIdType.MESH
F32, BF16 = jnp.float32, jnp.bfloat16

PIECES = (
    (0, 0, 1, 0),
    (0, 3, -1, 4),
    (0, 1, 0, 6),
    (1, 1, 1, 2),
    (1, 2, 0, 7),
    (0, 2, -1, 3),
    (1, 0, 1, 1),
    (1, 3, -1, 5),
)
USE = {0: (0, 0), 1: (1, 0), 2: (0, 1), 3: (1, 2), 4: (0, 3), 5: (1, 3), 6: (1, 1), 7: (0, 2)}


def nt(left, right):
    return lax.dot_general(left, right, (((1,), (1,)), ((), ())), preferred_element_type=F32)


def nn(left, right):
    return lax.dot_general(left, right, (((1,), (0,)), ((), ())), preferred_element_type=F32)


def terms(x, count):
    out = []
    for step in range(count):
        part = x.astype(BF16)
        out.append(part)
        if step < count - 1:
            x = x - part.astype(F32)
    return out


def stacked(x, count):
    return jnp.concatenate(terms(x, count), axis=0)


def folded(x, count):
    size = x.shape[0] // count
    total = x[:size]
    for step in range(1, count):
        total = total + x[step * size : (step + 1) * size]
    return total


def exact_nt(left, right, count):
    rows = left.shape[0]
    ls, rs = terms(left, count), terms(right, count)
    total = None
    for order in range(count):
        got = nt(jnp.concatenate(ls[: count - order], axis=0), rs[order])
        got = folded(got, count - order)
        total = got if total is None else total + got
    return total


def exact_nn(left, right, count):
    ls, rs = terms(left, count), terms(right, count)
    total = None
    for order in range(count):
        got = nn(jnp.concatenate(ls[: count - order], axis=0), rs[order])
        got = folded(got, count - order)
        total = got if total is None else total + got
    return total


def inverse_factors(grams):
    size = grams[0].shape[0]
    row = lax.broadcasted_iota(jnp.int32, (size, size), 0)
    col = lax.broadcasted_iota(jnp.int32, (size, size), 1)
    eye = (row == col).astype(F32)
    down = lax.broadcasted_iota(jnp.int32, (size, 1), 0)
    work = [jnp.concatenate([gram, eye], axis=1) for gram in grams]
    width = math.gcd(size, 8)
    for first in range(0, size, width):
        span = range(first, first + width)
        for n, a in enumerate(work):
            columns = {k: jnp.broadcast_to(a[:, k : k + 1], a.shape) for k in span}
            lines = {k: a[k : k + 1, :] for k in span}
            for k in span:
                factor = 1.0 / columns[k][k : k + 1, :]
                line = lines[k] * factor
                lead = jnp.where(down > k, columns[k], 0.0)
                for t in range(k + 1, first + width):
                    lines[t] = lines[t] - columns[k][t : t + 1, :] * line
                    columns[t] = columns[t] - lead * (columns[t][k : k + 1, :] * factor)
                a = a - lead * line
            work[n] = a
    out = []
    for a in work:
        diag = jnp.sum(jnp.where(row == col, a[:, :size], 0.0), axis=1, keepdims=True)
        out.append(a[:, size:] / jnp.sqrt(diag))
    return out


def kernel(
    g_size, b_size, ex, inv, coup, mask, sketch, bases_o, rc_o, re_o,
    ex_v, inv_v, c_v, sk_v, out_v, buf, src, skt, near, lin, lin_near, wbuf, v_out, v_in, bases_v, rc_v, re_v,
    load_sem, store_sem, p1_send, p1_recv, p1_fsend, p1_frecv, src_send, src_recv,
    sk_send, sk_recv, skp_send, skp_recv, v_send, v_recv, lin_send, lin_recv, w_send, w_recv,
):
    b, g = lax.axis_index("blk"), lax.axis_index("grp")
    has_left, has_right = b > 0, b < b_size - 1
    blocks, unknowns, _ = ex.shape
    rows = inv.shape[1]
    slots = coup.shape[1]
    r = sketch.shape[1]
    peers = [lax.rem(g + d, g_size) for d in range(1, g_size)]

    def load(number, source, target):
        return pltpu.make_async_copy(source, target, load_sem.at[number])

    loads = {}
    loads["sketch"] = load(0, sketch, sk_v)
    for i in range(blocks):
        loads["inv", i] = load(1 + 2 * i, inv.at[i], inv_v.at[i])
        loads["ex", i] = load(2 + 2 * i, ex.at[i], ex_v.at[i])
    for number, place in enumerate((7, 6, 0, 4, 2, 3, 1, 5)):
        i, k = USE[place]
        loads["c", i, k] = load(1 + 2 * blocks + number, coup.at[i, k], c_v.at[i, k])
    for name, copy in loads.items():
        if name[0] != "c":
            copy.start()

    barrier = pltpu.get_barrier_semaphore()

    @pl.when(has_left)
    def _():
        pl.semaphore_signal(barrier, inc=1, device_id=(b - 1, g), device_id_type=MESH)

    @pl.when(has_right)
    def _():
        pl.semaphore_signal(barrier, inc=1, device_id=(b + 1, g), device_id_type=MESH)

    for peer in peers:
        pl.semaphore_signal(barrier, inc=1, device_id=(b, peer), device_id_type=MESH)

    def remote(source, target, send, recv, device):
        return pltpu.make_async_remote_copy(
            src_ref=source, dst_ref=target, send_sem=send, recv_sem=recv,
            device_id=device, device_id_type=MESH,
        )

    def to_peers(source, target, send, recv):
        return [
            remote(source, target, send.at[d], recv.at[d], (b, peer)) for d, peer in enumerate(peers)
        ]

    def there(direction):
        return has_left if direction > 0 else has_right

    def sends(direction):
        return has_right if direction > 0 else has_left

    @pl.when(jnp.logical_not(has_left))
    def _():
        for p in range(g_size):
            buf[p, 0 : 3 * r, :] = jnp.zeros((3 * r, rows), F32)
        near[0] = jnp.zeros(near.shape[1:], F32)
        lin_near[0] = jnp.zeros(lin_near.shape[1:], F32)

    @pl.when(jnp.logical_not(has_right))
    def _():
        for p in range(g_size):
            buf[p, 3 * r : 6 * r, :] = jnp.zeros((3 * r, rows), F32)
        near[1] = jnp.zeros(near.shape[1:], F32)
        lin_near[1] = jnp.zeros(lin_near.shape[1:], F32)

    loads["sketch"].wait()
    order = list(range(1, slots + 1)) + [0]
    flat = jnp.concatenate([sk_v[k] for k in order], axis=0)
    flat_hi, flat_lo = terms(flat, 2)
    flat_both = jnp.concatenate([flat_hi, flat_lo], axis=0)

    piece_copies, own_copies = {}, {}

    def send_piece(block, slot, direction, place):
        here = buf.at[g, pl.ds(place * r, r)]
        if direction == 0:
            buf[g, pl.ds(place * r, r), :] = out_v[block, slot * r : (slot + 1) * r, :]
            own_copies[place] = to_peers(here, here, p1_fsend.at[place], p1_frecv.at[place])
            for copy in own_copies[place]:
                copy.start()
        else:
            copy = remote(
                out_v.at[block, pl.ds(slot * r, r)], here, p1_send.at[place], p1_recv.at[place],
                (b + direction, g),
            )
            piece_copies[place] = (direction, copy)
            pl.when(sends(direction))(copy.start)

    for i in range(blocks):
        loads["inv", i].wait()
        loads["ex", i].wait()
        if i == blocks - 1:
            for name, copy in loads.items():
                if name[0] == "c":
                    copy.start()
        primary = nn(inv_v[i], ex_v[i])
        primary_hi, primary_lo = terms(primary, 2)
        out_v[i] = folded(nt(flat_both, primary_hi), 2) + nt(flat_hi, primary_lo)
        if i == 0:
            neighbours = has_left.astype(jnp.int32) + has_right.astype(jnp.int32)
            pl.semaphore_wait(barrier, g_size - 1 + neighbours)
        for piece in PIECES[:3] if i == 0 else PIECES[3:]:
            send_piece(*piece)

    def coupled(i, k, parts):
        total = None
        for p in range(g_size):
            got = nt(stacked(parts[p], 3), c_v[i, k, :, p * rows : (p + 1) * rows])
            total = got if total is None else total + got
        return folded(total, 3)

    weights = [[mask[i, k].astype(F32) for k in range(slots)] for i in range(blocks)]
    sources = [None] * blocks

    def add_source(place):
        i, k = USE[place]
        loads["c", i, k].wait()
        term = weights[i][k] * coupled(i, k, [buf[p, place * r : (place + 1) * r, :] for p in range(g_size)])
        sources[i] = term if sources[i] is None else sources[i] + term

    def forward(places):
        for place in places:
            direction, copy = piece_copies[place]
            here = buf.at[g, pl.ds(place * r, r)]
            own_copies[place] = to_peers(here, here, p1_fsend.at[place], p1_frecv.at[place])

            @pl.when(there(direction))
            def _():
                copy.wait_recv()
                for out in own_copies[place]:
                    out.start()

    def arrived(place):
        if place in piece_copies:

            @pl.when(there(piece_copies[place][0]))
            def _():
                for out in own_copies[place]:
                    out.wait_recv()
        else:
            for out in own_copies[place]:
                out.wait_recv()

    src_copies, sk_copies, skp_copies, v_copies = {}, {}, {}, {}

    def finish_source(i):
        src[g, i * r : (i + 1) * r, :] = sources[i]
        here = src.at[g, pl.ds(i * r, r)]
        src_copies[i] = to_peers(here, here, src_send.at[i], src_recv.at[i])
        for copy in src_copies[i]:
            copy.start()

    def sketch_block(i):
        for copy in src_copies[i]:
            copy.wait_recv()
        total = None
        for p in range(g_size):
            got = nt(
                stacked(src[p, i * r : (i + 1) * r, :], 3), inv_v[i, :, p * rows : (p + 1) * rows]
            )
            total = got if total is None else total + got
        skt[g, i * r : (i + 1) * r, :] = out_v[i, slots * r : (slots + 1) * r, :] - folded(total, 3)
        here = skt.at[g, pl.ds(i * r, r)]
        for side, direction in enumerate((1, -1)):
            copy = remote(
                here, near.at[side, pl.ds(i * r, r)], sk_send.at[side, i], sk_recv.at[side, i],
                (b + direction, g),
            )
            sk_copies[side, i] = (direction, copy)
            pl.when(sends(direction))(copy.start)
        skp_copies[i] = to_peers(here, here, skp_send.at[i], skp_recv.at[i])
        for copy in skp_copies[i]:
            copy.start()

    def project(i, k):
        got = folded(nn(stacked(skt[g, i * r : (i + 1) * r, :], 3), c_v[i, k]), 3)
        for p in range(g_size):
            v_out[p, (i * slots + k) * r : (i * slots + k + 1) * r, :] = got[:, p * rows : (p + 1) * rows]

    def send_projected(i):
        span = pl.ds(i * slots * r, slots * r)
        v_copies[i] = [
            remote(
                v_out.at[peer, span], v_in.at[d, span], v_send.at[i, d], v_recv.at[i, d], (b, peer)
            )
            for d, peer in enumerate(peers)
        ]
        for copy in v_copies[i]:
            copy.start()

    for place in (7, 6):
        arrived(place)
        add_source(place)
    forward((0, 4))
    arrived(0)
    add_source(0)
    forward((2,))
    arrived(4)
    add_source(4)
    arrived(2)
    add_source(2)
    finish_source(0)
    forward((3,))
    sketch_block(0)
    forward((1, 5))
    arrived(3)
    add_source(3)
    arrived(1)
    add_source(1)
    arrived(5)
    add_source(5)
    finish_source(1)
    for k in range(slots):
        project(0, k)
    send_projected(0)
    sketch_block(1)

    for i in range(blocks):
        for copy in skp_copies[i]:
            copy.wait_recv()
    grams = []
    for i in range(blocks):
        total = None
        for p in range(g_size):
            part = skt[p, i * r : (i + 1) * r, :]
            got = exact_nt(part, part, 3)
            total = got if total is None else total + got
        grams.append(total * (1.0 / unknowns))
    for k in range(slots):
        project(1, k)
    inverses = inverse_factors(grams)
    for i in range(blocks):
        lin[i * r : (i + 1) * r, :] = jnp.concatenate([inverses[i]] * slots, axis=1)
    lin_copies = []
    for side, direction in enumerate((1, -1)):
        copy = remote(lin, lin_near.at[side], lin_send.at[side], lin_recv.at[side], (b + direction, g))
        lin_copies.append((direction, copy))
        pl.when(sends(direction))(copy.start)

    send_projected(1)

    wide = slots * r
    row = lax.broadcasted_iota(jnp.int32, (wide, wide), 0) // r
    col = lax.broadcasted_iota(jnp.int32, (wide, wide), 1) // r
    diagonal = row == col
    projected = []
    for i in range(blocks):
        for copy in v_copies[i]:
            copy.wait_recv()
        span = slice(i * wide, (i + 1) * wide)
        total = v_out[g, pl.ds(i * wide, wide), :]
        for d in range(g_size - 1):
            total = total + v_in[d, span, :]
        factors = jnp.where(diagonal, jnp.concatenate([lin[i * r : (i + 1) * r, :]] * slots, axis=0), 0.0)
        projected.append(exact_nn(factors, total, 3))

    products = {}

    def reduce(users, basis):
        left = [projected[i][k * r : (k + 1) * r] for i, k in users]
        got = exact_nt(left[0] if len(left) == 1 else jnp.concatenate(left, axis=0), basis, 3)
        for n, user in enumerate(users):
            products[user] = got[n * r : (n + 1) * r]

    reduce([(1, 1)], skt[g, 0:r, :])
    reduce([(0, 2)], skt[g, r : 2 * r, :])
    for i, side, users in (
        (0, 0, [(0, 0)]),
        (0, 1, [(0, 3), (1, 2)]),
        (1, 0, [(0, 1), (1, 0)]),
        (1, 1, [(1, 3)]),
    ):
        direction, copy = sk_copies[side, i]
        pl.when(there(direction))(copy.wait_recv)
        reduce(users, near[side, i * r : (i + 1) * r, :])
    for i in range(blocks):
        wbuf[g, i * r : (i + 1) * r, :] = jnp.concatenate([products[i, k] for k in range(slots)], axis=1)
    here = wbuf.at[g]
    w_copies = to_peers(here, here, w_send, w_recv)
    for copy in w_copies:
        copy.start()

    scale = 1.0 / math.sqrt(unknowns)
    for i in range(blocks):
        bases_v[i] = exact_nn(inverses[i], skt[g, i * r : (i + 1) * r, :], 3)
        driven = None
        for p in range(g_size):
            got = nn(stacked(skt[p, i * r : (i + 1) * r, :], 3), ex_v[i, p * rows : (p + 1) * rows, :])
            driven = got if driven is None else driven + got
        re_v[i] = exact_nn(inverses[i], folded(driven, 3), 3) * scale
    stores = [
        pltpu.make_async_copy(bases_v, bases_o, store_sem.at[0]),
        pltpu.make_async_copy(re_v, re_o, store_sem.at[1]),
    ]
    for copy in stores:
        copy.start()

    for direction, copy in lin_copies:
        pl.when(there(direction))(copy.wait_recv)
    for copy in w_copies:
        copy.wait_recv()
    total = wbuf[0]
    for p in range(1, g_size):
        total = total + wbuf[p]
    left_a, left_b = lin_near[0, 0:r, :], lin_near[0, r : 2 * r, :]
    right_a, right_b = lin_near[1, 0:r, :], lin_near[1, r : 2 * r, :]
    own_a, own_b = lin[0:r, :], lin[r : 2 * r, :]
    beside = ((left_a, left_b, own_b, right_a), (left_b, own_a, right_a, right_b))
    for i in range(blocks):
        factors = jnp.where(diagonal, jnp.concatenate(beside[i], axis=0), 0.0)
        got = exact_nt(total[i * r : (i + 1) * r], factors, 3) * scale
        for k in range(slots):
            rc_v[i, k] = got[:, k * r : (k + 1) * r]
    last = pltpu.make_async_copy(rc_v, rc_o, store_sem.at[2])
    last.start()

    for direction, copy in list(piece_copies.values()) + list(sk_copies.values()) + lin_copies:
        pl.when(sends(direction))(copy.wait_send)
    for place, copies in own_copies.items():
        for copy in copies:
            if place in piece_copies:
                pl.when(there(piece_copies[place][0]))(copy.wait_send)
            else:
                copy.wait_send()
    for copies in list(src_copies.values()) + list(skp_copies.values()) + list(v_copies.values()) + [w_copies]:
        for copy in copies:
            copy.wait_send()
    for copy in stores:
        copy.wait()
    last.wait()


def shards(g_size, b_size, excitation, inverse_self, coupling, neighbour_mask, sketch):
    blocks, unknowns, columns = excitation.shape
    rows = inverse_self.shape[1]
    slots = coupling.shape[1]
    sketch = jnp.swapaxes(sketch, 1, 2)
    r = sketch.shape[1]
    assert blocks == 2 and slots == 4 and rows * g_size == unknowns
    others = max(g_size - 1, 1)
    wide = slots * r
    vmem = lambda *shape: pltpu.VMEM(shape, F32)
    dma = lambda *shape: pltpu.SemaphoreType.DMA(shape)
    anywhere = pl.BlockSpec(memory_space=pl.ANY)
    flops = 2 * blocks * rows * unknowns * (columns + 2 * slots * 3 * r)
    bases, reduced, driven = pl.pallas_call(
        functools.partial(kernel, g_size, b_size),
        out_shape=(
            jax.ShapeDtypeStruct((blocks, r, rows), F32),
            jax.ShapeDtypeStruct((blocks, slots, r, r), F32),
            jax.ShapeDtypeStruct((blocks, r, columns), F32),
        ),
        in_specs=[anywhere, anywhere, anywhere, pl.BlockSpec(memory_space=pltpu.SMEM), anywhere],
        out_specs=(anywhere, anywhere, anywhere),
        scratch_shapes=[
            pltpu.VMEM(excitation.shape, BF16),
            pltpu.VMEM(inverse_self.shape, BF16),
            pltpu.VMEM(coupling.shape, BF16),
            vmem(*sketch.shape),
            vmem(blocks, (slots + 1) * r, rows),
            vmem(g_size, 8 * r, rows),
            vmem(g_size, 2 * r, rows),
            vmem(g_size, 2 * r, rows),
            vmem(2, 2 * r, rows),
            vmem(2 * r, wide),
            vmem(2, 2 * r, wide),
            vmem(g_size, 2 * r, wide),
            vmem(g_size, blocks * wide, rows),
            vmem(others, blocks * wide, rows),
            vmem(blocks, r, rows),
            vmem(blocks, slots, r, r),
            vmem(blocks, r, columns),
            dma(1 + 2 * blocks + blocks * slots),
            dma(3),
            dma(6),
            dma(6),
            dma(8, others),
            dma(8, others),
            dma(blocks, others),
            dma(blocks, others),
            dma(2, blocks),
            dma(2, blocks),
            dma(blocks, others),
            dma(blocks, others),
            dma(blocks, others),
            dma(blocks, others),
            dma(2),
            dma(2),
            dma(others),
            dma(others),
        ],
        compiler_params=pltpu.CompilerParams(
            collective_id=0, has_side_effects=True, vmem_limit_bytes=60 * 1024 * 1024
        ),
        cost_estimate=pl.CostEstimate(
            flops=flops, bytes_accessed=2 * (coupling.size + inverse_self.size), transcendentals=0
        ),
        name="basis_currents",
    )(excitation, inverse_self, coupling, neighbour_mask, sketch)
    return jnp.swapaxes(bases, 1, 2), reduced, driven


def solution(mesh):
    return jax.shard_map(
        functools.partial(shards, mesh.shape["grp"], mesh.shape["blk"]),
        mesh=mesh,
        in_specs=(
            P("blk", None, None),
            P("blk", "grp", None),
            P("blk", None, "grp", None),
            P("blk", None),
            P(),
        ),
        out_specs=(P("blk", "grp", None), P("blk", None, None, None), P("blk", None, None)),
        check_vma=False,
    )
```

```python
import functools
import math

import jax
import jax.numpy as jnp
from jax import lax
from jax.experimental import pallas as pl
from jax.experimental.pallas import tpu as pltpu
from jax.sharding import PartitionSpec as P

MESH = pl.DeviceIdType.MESH
F32, BF16 = jnp.float32, jnp.bfloat16

PIECES = (
    (0, 0, 1, 0),
    (0, 3, -1, 4),
    (0, 1, 0, 6),
    (1, 1, 1, 2),
    (1, 2, 0, 7),
)
LATER = (((0, 2, -1, 3), 4), ((1, 0, 1, 1), 0), ((1, 3, -1, 5), 2))
USE = {0: (0, 0), 1: (1, 0), 2: (0, 1), 3: (1, 2), 4: (0, 3), 5: (1, 3), 6: (1, 1), 7: (0, 2)}


def nt(left, right):
    return lax.dot_general(left, right, (((1,), (1,)), ((), ())), preferred_element_type=F32)


def nn(left, right):
    return lax.dot_general(left, right, (((1,), (0,)), ((), ())), preferred_element_type=F32)


def terms(x, count):
    out = []
    for step in range(count):
        part = x.astype(BF16)
        out.append(part)
        if step < count - 1:
            x = x - part.astype(F32)
    return out


def stacked(x, count):
    return jnp.concatenate(terms(x, count), axis=0)


def folded(x, count):
    size = x.shape[0] // count
    total = x[:size]
    for step in range(1, count):
        total = total + x[step * size : (step + 1) * size]
    return total


def exact_nt(left, right, count):
    rows = left.shape[0]
    ls, rs = terms(left, count), terms(right, count)
    total = None
    for order in range(count):
        got = nt(jnp.concatenate(ls[: count - order], axis=0), rs[order])
        got = folded(got, count - order)
        total = got if total is None else total + got
    return total


def exact_nn(left, right, count):
    ls, rs = terms(left, count), terms(right, count)
    total = None
    for order in range(count):
        got = nn(jnp.concatenate(ls[: count - order], axis=0), rs[order])
        got = folded(got, count - order)
        total = got if total is None else total + got
    return total


def inverse_factors(grams):
    size = grams[0].shape[0]
    row = lax.broadcasted_iota(jnp.int32, (size, size), 0)
    col = lax.broadcasted_iota(jnp.int32, (size, size), 1)
    eye = (row == col).astype(F32)
    down = lax.broadcasted_iota(jnp.int32, (size, 1), 0)
    work = [jnp.concatenate([gram, eye], axis=1) for gram in grams]
    width = math.gcd(size, 8)
    for first in range(0, size, width):
        span = range(first, first + width)
        for n, a in enumerate(work):
            columns = {k: jnp.broadcast_to(a[:, k : k + 1], a.shape) for k in span}
            lines = {k: a[k : k + 1, :] for k in span}
            for k in span:
                factor = 1.0 / columns[k][k : k + 1, :]
                line = lines[k] * factor
                lead = jnp.where(down > k, columns[k], 0.0)
                for t in range(k + 1, first + width):
                    lines[t] = lines[t] - columns[k][t : t + 1, :] * line
                    columns[t] = columns[t] - lead * (columns[t][k : k + 1, :] * factor)
                a = a - lead * line
            work[n] = a
    out = []
    for a in work:
        diag = jnp.sum(jnp.where(row == col, a[:, :size], 0.0), axis=1, keepdims=True)
        out.append(a[:, size:] / jnp.sqrt(diag))
    return out


def kernel(
    g_size, b_size, ex, inv, coup, mask, sketch, bases_o, rc_o, re_o,
    ex_v, inv_v, c_v, sk_v, out_v, buf, src, skt, near, lin, lin_near, wbuf, v_out, v_in, mask_s,
    load_sem, p1_send, p1_recv, p1_fsend, p1_frecv, src_send, src_recv,
    sk_send, sk_recv, skp_send, skp_recv, v_send, v_recv, lin_send, lin_recv, w_send, w_recv,
):
    b, g = lax.axis_index("blk"), lax.axis_index("grp")
    has_left, has_right = b > 0, b < b_size - 1
    blocks, unknowns, _ = ex.shape
    rows = inv.shape[1]
    slots = coup.shape[1]
    r = sketch.shape[1]
    peers = [lax.rem(g + d, g_size) for d in range(1, g_size)]

    def load(number, source, target):
        return pltpu.make_async_copy(source, target, load_sem.at[number])

    loads = {}
    loads["sketch"] = load(0, sketch, sk_v)
    loads["mask"] = load(1 + 2 * blocks + blocks * slots, mask, mask_s)
    for i in range(blocks):
        loads["inv", i] = load(1 + 2 * i, inv.at[i], inv_v.at[i])
        loads["ex", i] = load(2 + 2 * i, ex.at[i], ex_v.at[i])
    for number, place in enumerate((7, 6, 0, 4, 2, 3, 1, 5)):
        i, k = USE[place]
        loads["c", i, k] = load(1 + 2 * blocks + number, coup.at[i, k], c_v.at[i, k])
    for name, copy in loads.items():
        if name[0] != "c":
            copy.start()

    barrier = pltpu.get_barrier_semaphore()

    @pl.when(has_left)
    def _():
        pl.semaphore_signal(barrier, inc=1, device_id=(b - 1, g), device_id_type=MESH)

    @pl.when(has_right)
    def _():
        pl.semaphore_signal(barrier, inc=1, device_id=(b + 1, g), device_id_type=MESH)

    for peer in peers:
        pl.semaphore_signal(barrier, inc=1, device_id=(b, peer), device_id_type=MESH)

    def remote(source, target, send, recv, device):
        return pltpu.make_async_remote_copy(
            src_ref=source, dst_ref=target, send_sem=send, recv_sem=recv,
            device_id=device, device_id_type=MESH,
        )

    def to_peers(source, target, send, recv):
        return [
            remote(source, target, send.at[d], recv.at[d], (b, peer)) for d, peer in enumerate(peers)
        ]

    def there(direction):
        return has_left if direction > 0 else has_right

    def sends(direction):
        return has_right if direction > 0 else has_left

    @pl.when(jnp.logical_not(has_left))
    def _():
        for p in range(g_size):
            buf[p, 0 : 3 * r, :] = jnp.zeros((3 * r, rows), F32)
        near[0] = jnp.zeros(near.shape[1:], F32)
        lin_near[0] = jnp.zeros(lin_near.shape[1:], F32)

    @pl.when(jnp.logical_not(has_right))
    def _():
        for p in range(g_size):
            buf[p, 3 * r : 6 * r, :] = jnp.zeros((3 * r, rows), F32)
        near[1] = jnp.zeros(near.shape[1:], F32)
        lin_near[1] = jnp.zeros(lin_near.shape[1:], F32)

    loads["sketch"].wait()
    order = list(range(1, slots + 1)) + [0]
    flat = jnp.concatenate([sk_v[k] for k in order], axis=0)
    flat_hi, flat_lo = terms(flat, 2)
    flat_both = jnp.concatenate([flat_hi, flat_lo], axis=0)

    piece_copies, own_copies = {}, {}

    def send_piece(block, slot, direction, place):
        here = buf.at[g, pl.ds(place * r, r)]
        if direction == 0:
            buf[g, pl.ds(place * r, r), :] = out_v[block, slot * r : (slot + 1) * r, :]
            own_copies[place] = to_peers(here, here, p1_fsend.at[place], p1_frecv.at[place])
            for copy in own_copies[place]:
                copy.start()
        else:
            copy = remote(
                out_v.at[block, pl.ds(slot * r, r)], here, p1_send.at[place], p1_recv.at[place],
                (b + direction, g),
            )
            piece_copies[place] = (direction, copy)
            pl.when(sends(direction))(copy.start)

    for i in range(blocks):
        loads["inv", i].wait()
        loads["ex", i].wait()
        if i == blocks - 1:
            for name, copy in loads.items():
                if name[0] == "c":
                    copy.start()
        primary = nn(inv_v[i], ex_v[i])
        primary_hi, primary_lo = terms(primary, 2)
        out_v[i] = folded(nt(flat_both, primary_hi), 2) + nt(flat_hi, primary_lo)
        if i == 0:
            neighbours = has_left.astype(jnp.int32) + has_right.astype(jnp.int32)
            pl.semaphore_wait(barrier, g_size - 1 + neighbours)
        for piece in PIECES[:3] if i == 0 else PIECES[3:]:
            send_piece(*piece)

    def coupled(i, k, parts):
        total = None
        for p in range(g_size):
            got = nt(stacked(parts[p], 3), c_v[i, k, :, p * rows : (p + 1) * rows])
            total = got if total is None else total + got
        return folded(total, 3)

    loads["mask"].wait()
    weights = [[mask_s[i, k].astype(F32) for k in range(slots)] for i in range(blocks)]
    sources = [None] * blocks

    def add_source(place):
        i, k = USE[place]
        loads["c", i, k].wait()
        term = weights[i][k] * coupled(i, k, [buf[p, place * r : (place + 1) * r, :] for p in range(g_size)])
        sources[i] = term if sources[i] is None else sources[i] + term

    def forward(places):
        for place in places:
            direction, copy = piece_copies[place]
            here = buf.at[g, pl.ds(place * r, r)]
            own_copies[place] = to_peers(here, here, p1_fsend.at[place], p1_frecv.at[place])

            @pl.when(there(direction))
            def _():
                copy.wait_recv()
                for out in own_copies[place]:
                    out.start()

    def arrived(place):
        if place in piece_copies:

            @pl.when(there(piece_copies[place][0]))
            def _():
                for out in own_copies[place]:
                    out.wait_recv()
        else:
            for out in own_copies[place]:
                out.wait_recv()

    src_copies, sk_copies, skp_copies, v_copies = {}, {}, {}, {}

    def finish_source(i):
        src[g, i * r : (i + 1) * r, :] = sources[i]
        here = src.at[g, pl.ds(i * r, r)]
        src_copies[i] = to_peers(here, here, src_send.at[i], src_recv.at[i])
        for copy in src_copies[i]:
            copy.start()

    def sketch_block(i):
        for copy in src_copies[i]:
            copy.wait_recv()
        total = None
        for p in range(g_size):
            got = nt(
                stacked(src[p, i * r : (i + 1) * r, :], 3), inv_v[i, :, p * rows : (p + 1) * rows]
            )
            total = got if total is None else total + got
        skt[g, i * r : (i + 1) * r, :] = out_v[i, slots * r : (slots + 1) * r, :] - folded(total, 3)
        here = skt.at[g, pl.ds(i * r, r)]
        for side, direction in enumerate((1, -1)):
            copy = remote(
                here, near.at[side, pl.ds(i * r, r)], sk_send.at[side, i], sk_recv.at[side, i],
                (b + direction, g),
            )
            sk_copies[side, i] = (direction, copy)
            pl.when(sends(direction))(copy.start)
        skp_copies[i] = to_peers(here, here, skp_send.at[i], skp_recv.at[i])
        for copy in skp_copies[i]:
            copy.start()

    def project(i, k):
        got = folded(nn(stacked(skt[g, i * r : (i + 1) * r, :], 3), c_v[i, k]), 3)
        for p in range(g_size):
            v_out[p, (i * slots + k) * r : (i * slots + k + 1) * r, :] = got[:, p * rows : (p + 1) * rows]

    def send_projected(i):
        span = pl.ds(i * slots * r, slots * r)
        v_copies[i] = [
            remote(
                v_out.at[peer, span], v_in.at[d, span], v_send.at[i, d], v_recv.at[i, d], (b, peer)
            )
            for d, peer in enumerate(peers)
        ]
        for copy in v_copies[i]:
            copy.start()

    for place in (7, 6):
        arrived(place)
        add_source(place)
    for piece, first in LATER:
        direction, copy = piece_copies[first]
        pl.when(sends(direction))(copy.wait_send)
        send_piece(*piece)
    forward((0, 4))
    arrived(0)
    add_source(0)
    forward((2,))
    arrived(4)
    add_source(4)
    arrived(2)
    add_source(2)
    finish_source(0)
    forward((3,))
    sketch_block(0)
    forward((1, 5))
    arrived(3)
    add_source(3)
    arrived(1)
    add_source(1)
    arrived(5)
    add_source(5)
    finish_source(1)
    for k in range(slots):
        project(0, k)
    send_projected(0)
    sketch_block(1)

    for i in range(blocks):
        for copy in skp_copies[i]:
            copy.wait_recv()
    grams = []
    for i in range(blocks):
        total = None
        for p in range(g_size):
            part = skt[p, i * r : (i + 1) * r, :]
            got = exact_nt(part, part, 3)
            total = got if total is None else total + got
        grams.append(total * (1.0 / unknowns))
    for k in range(slots):
        project(1, k)
    inverses = inverse_factors(grams)
    for i in range(blocks):
        lin[i * r : (i + 1) * r, :] = jnp.concatenate([inverses[i]] * slots, axis=1)
    lin_copies = []
    for side, direction in enumerate((1, -1)):
        copy = remote(lin, lin_near.at[side], lin_send.at[side], lin_recv.at[side], (b + direction, g))
        lin_copies.append((direction, copy))
        pl.when(sends(direction))(copy.start)

    send_projected(1)

    wide = slots * r
    row = lax.broadcasted_iota(jnp.int32, (wide, wide), 0) // r
    col = lax.broadcasted_iota(jnp.int32, (wide, wide), 1) // r
    diagonal = row == col
    projected = []
    for i in range(blocks):
        for copy in v_copies[i]:
            copy.wait_recv()
        span = slice(i * wide, (i + 1) * wide)
        total = v_out[g, pl.ds(i * wide, wide), :]
        for d in range(g_size - 1):
            total = total + v_in[d, span, :]
        factors = jnp.where(diagonal, jnp.concatenate([lin[i * r : (i + 1) * r, :]] * slots, axis=0), 0.0)
        projected.append(exact_nn(factors, total, 3))

    products = {}

    def reduce(users, basis):
        left = [projected[i][k * r : (k + 1) * r] for i, k in users]
        got = exact_nt(left[0] if len(left) == 1 else jnp.concatenate(left, axis=0), basis, 3)
        for n, user in enumerate(users):
            products[user] = got[n * r : (n + 1) * r]

    reduce([(1, 1)], skt[g, 0:r, :])
    reduce([(0, 2)], skt[g, r : 2 * r, :])
    for i, side, users in (
        (0, 0, [(0, 0)]),
        (0, 1, [(0, 3), (1, 2)]),
        (1, 0, [(0, 1), (1, 0)]),
        (1, 1, [(1, 3)]),
    ):
        direction, copy = sk_copies[side, i]
        pl.when(there(direction))(copy.wait_recv)
        reduce(users, near[side, i * r : (i + 1) * r, :])
    for i in range(blocks):
        wbuf[g, i * r : (i + 1) * r, :] = jnp.concatenate([products[i, k] for k in range(slots)], axis=1)
    here = wbuf.at[g]
    w_copies = to_peers(here, here, w_send, w_recv)
    for copy in w_copies:
        copy.start()

    scale = 1.0 / math.sqrt(unknowns)
    for i in range(blocks):
        bases_o[i] = exact_nn(inverses[i], skt[g, i * r : (i + 1) * r, :], 3)
        driven = None
        for p in range(g_size):
            got = nn(stacked(skt[p, i * r : (i + 1) * r, :], 3), ex_v[i, p * rows : (p + 1) * rows, :])
            driven = got if driven is None else driven + got
        re_o[i] = exact_nn(inverses[i], folded(driven, 3), 3) * scale
    for direction, copy in lin_copies:
        pl.when(there(direction))(copy.wait_recv)
    for copy in w_copies:
        copy.wait_recv()
    total = wbuf[0]
    for p in range(1, g_size):
        total = total + wbuf[p]
    left_a, left_b = lin_near[0, 0:r, :], lin_near[0, r : 2 * r, :]
    right_a, right_b = lin_near[1, 0:r, :], lin_near[1, r : 2 * r, :]
    own_a, own_b = lin[0:r, :], lin[r : 2 * r, :]
    beside = ((left_a, left_b, own_b, right_a), (left_b, own_a, right_a, right_b))
    for i in range(blocks):
        factors = jnp.where(diagonal, jnp.concatenate(beside[i], axis=0), 0.0)
        got = exact_nt(total[i * r : (i + 1) * r], factors, 3) * scale
        for k in range(slots):
            rc_o[i, k] = got[:, k * r : (k + 1) * r]

    waited = [first for _, first in LATER]
    last_pieces = [pair for place, pair in piece_copies.items() if place not in waited]
    for direction, copy in last_pieces + list(sk_copies.values()) + lin_copies:
        pl.when(sends(direction))(copy.wait_send)
    for place, copies in own_copies.items():
        for copy in copies:
            if place in piece_copies:
                pl.when(there(piece_copies[place][0]))(copy.wait_send)
            else:
                copy.wait_send()
    for copies in list(src_copies.values()) + list(skp_copies.values()) + list(v_copies.values()) + [w_copies]:
        for copy in copies:
            copy.wait_send()


def shards(g_size, b_size, excitation, inverse_self, coupling, neighbour_mask, sketch):
    blocks, unknowns, columns = excitation.shape
    rows = inverse_self.shape[1]
    slots = coupling.shape[1]
    sketch = jnp.swapaxes(sketch, 1, 2)
    r = sketch.shape[1]
    assert blocks == 2 and slots == 4 and rows * g_size == unknowns
    others = max(g_size - 1, 1)
    wide = slots * r
    vmem = lambda *shape: pltpu.VMEM(shape, F32)
    dma = lambda *shape: pltpu.SemaphoreType.DMA(shape)
    anywhere = pl.BlockSpec(memory_space=pl.ANY)
    flops = 2 * blocks * rows * unknowns * (columns + 2 * slots * 3 * r)
    bases, reduced, driven = pl.pallas_call(
        functools.partial(kernel, g_size, b_size),
        out_shape=(vmem(blocks, r, rows), vmem(blocks, slots, r, r), vmem(blocks, r, columns)),
        in_specs=[anywhere] * 5,
        out_specs=(pl.BlockSpec(memory_space=pltpu.VMEM),) * 3,
        scratch_shapes=[
            pltpu.VMEM(excitation.shape, BF16),
            pltpu.VMEM(inverse_self.shape, BF16),
            pltpu.VMEM(coupling.shape, BF16),
            vmem(*sketch.shape),
            vmem(blocks, (slots + 1) * r, rows),
            vmem(g_size, 8 * r, rows),
            vmem(g_size, 2 * r, rows),
            vmem(g_size, 2 * r, rows),
            vmem(2, 2 * r, rows),
            vmem(2 * r, wide),
            vmem(2, 2 * r, wide),
            vmem(g_size, 2 * r, wide),
            vmem(g_size, blocks * wide, rows),
            vmem(others, blocks * wide, rows),
            pltpu.SMEM(neighbour_mask.shape, neighbour_mask.dtype),
            dma(2 + 2 * blocks + blocks * slots),
            dma(6),
            dma(6),
            dma(8, others),
            dma(8, others),
            dma(blocks, others),
            dma(blocks, others),
            dma(2, blocks),
            dma(2, blocks),
            dma(blocks, others),
            dma(blocks, others),
            dma(blocks, others),
            dma(blocks, others),
            dma(2),
            dma(2),
            dma(others),
            dma(others),
        ],
        compiler_params=pltpu.CompilerParams(
            collective_id=0, has_side_effects=True, vmem_limit_bytes=60 * 1024 * 1024
        ),
        cost_estimate=pl.CostEstimate(
            flops=flops, bytes_accessed=2 * (coupling.size + inverse_self.size), transcendentals=0
        ),
        name="basis_currents",
    )(excitation, inverse_self, coupling, neighbour_mask, sketch)
    return jnp.swapaxes(bases, 1, 2), reduced, driven


def solution(mesh):
    return jax.shard_map(
        functools.partial(shards, mesh.shape["grp"], mesh.shape["blk"]),
        mesh=mesh,
        in_specs=(
            P("blk", None, None),
            P("blk", "grp", None),
            P("blk", None, "grp", None),
            P("blk", None),
            P(),
        ),
        out_specs=(P("blk", "grp", None), P("blk", None, None, None), P("blk", None, None)),
        check_vma=False,
    )
```

```python
import functools
import math

import jax
import jax.numpy as jnp
from jax import lax
from jax.experimental import pallas as pl
from jax.experimental.pallas import tpu as pltpu
from jax.sharding import PartitionSpec as P

MESH = pl.DeviceIdType.MESH
F32, BF16 = jnp.float32, jnp.bfloat16

PIECES = (
    (0, 0, 1, 0),
    (0, 3, -1, 4),
    (0, 1, 0, 6),
    (1, 1, 1, 2),
    (1, 2, 0, 7),
)
LATER = (((0, 2, -1, 3), 4), ((1, 0, 1, 1), 0), ((1, 3, -1, 5), 2))
USE = {0: (0, 0), 1: (1, 0), 2: (0, 1), 3: (1, 2), 4: (0, 3), 5: (1, 3), 6: (1, 1), 7: (0, 2)}


def nt(left, right):
    return lax.dot_general(left, right, (((1,), (1,)), ((), ())), preferred_element_type=F32)


def nn(left, right):
    return lax.dot_general(left, right, (((1,), (0,)), ((), ())), preferred_element_type=F32)


def terms(x, count):
    out = []
    for step in range(count):
        part = x.astype(BF16)
        out.append(part)
        if step < count - 1:
            x = x - part.astype(F32)
    return out


def stacked(x, count):
    return jnp.concatenate(terms(x, count), axis=0)


def folded(x, count):
    size = x.shape[0] // count
    total = x[:size]
    for step in range(1, count):
        total = total + x[step * size : (step + 1) * size]
    return total


def exact_nt(left, right, count):
    rows = left.shape[0]
    ls, rs = terms(left, count), terms(right, count)
    total = None
    for order in range(count):
        got = nt(jnp.concatenate(ls[: count - order], axis=0), rs[order])
        got = folded(got, count - order)
        total = got if total is None else total + got
    return total


def exact_nn(left, right, count):
    ls, rs = terms(left, count), terms(right, count)
    total = None
    for order in range(count):
        got = nn(jnp.concatenate(ls[: count - order], axis=0), rs[order])
        got = folded(got, count - order)
        total = got if total is None else total + got
    return total


def inverse_factors(grams):
    size = grams[0].shape[0]
    row = lax.broadcasted_iota(jnp.int32, (size, size), 0)
    col = lax.broadcasted_iota(jnp.int32, (size, size), 1)
    eye = (row == col).astype(F32)
    down = lax.broadcasted_iota(jnp.int32, (size, 1), 0)
    work = [jnp.concatenate([gram, eye], axis=1) for gram in grams]
    width = math.gcd(size, 8)
    for first in range(0, size, width):
        span = range(first, first + width)
        for n, a in enumerate(work):
            columns = {k: jnp.broadcast_to(a[:, k : k + 1], a.shape) for k in span}
            lines = {k: a[k : k + 1, :] for k in span}
            for k in span:
                factor = 1.0 / columns[k][k : k + 1, :]
                line = lines[k] * factor
                lead = jnp.where(down > k, columns[k], 0.0)
                for t in range(k + 1, first + width):
                    lines[t] = lines[t] - columns[k][t : t + 1, :] * line
                    columns[t] = columns[t] - lead * (columns[t][k : k + 1, :] * factor)
                a = a - lead * line
            work[n] = a
    out = []
    for a in work:
        diag = jnp.sum(jnp.where(row == col, a[:, :size], 0.0), axis=1, keepdims=True)
        out.append(a[:, size:] / jnp.sqrt(diag))
    return out


def kernel(
    g_size, b_size, ex, inv, coup, mask, sketch, bases_o, rc_o, re_o,
    ex_v, inv_v, c_v, sk_v, out_v, buf, src, skt, near, lin, lin_near, wbuf, v_out, v_in, mask_s,
    load_sem, p1_send, p1_recv, p1_fsend, p1_frecv, src_send, src_recv,
    sk_send, sk_recv, skp_send, skp_recv, v_send, v_recv, lin_send, lin_recv, w_send, w_recv,
):
    b, g = lax.axis_index("blk"), lax.axis_index("grp")
    has_left, has_right = b > 0, b < b_size - 1
    blocks, unknowns, _ = ex.shape
    rows = inv.shape[1]
    slots = coup.shape[1]
    r = sketch.shape[1]
    peers = [lax.rem(g + d, g_size) for d in range(1, g_size)]

    def load(number, source, target):
        return pltpu.make_async_copy(source, target, load_sem.at[number])

    loads = {}
    loads["sketch"] = load(0, sketch, sk_v)
    loads["mask"] = load(1 + 2 * blocks + blocks * slots, mask, mask_s)
    for i in range(blocks):
        loads["inv", i] = load(1 + 2 * i, inv.at[i], inv_v.at[i])
        loads["ex", i] = load(2 + 2 * i, ex.at[i], ex_v.at[i])
    for number, place in enumerate((7, 6, 0, 4, 2, 3, 1, 5)):
        i, k = USE[place]
        loads["c", i, k] = load(1 + 2 * blocks + number, coup.at[i, k], c_v.at[i, k])
    for name, copy in loads.items():
        if name[0] != "c":
            copy.start()

    barrier = pltpu.get_barrier_semaphore()

    @pl.when(has_left)
    def _():
        pl.semaphore_signal(barrier, inc=1, device_id=(b - 1, g), device_id_type=MESH)

    @pl.when(has_right)
    def _():
        pl.semaphore_signal(barrier, inc=1, device_id=(b + 1, g), device_id_type=MESH)

    for peer in peers:
        pl.semaphore_signal(barrier, inc=1, device_id=(b, peer), device_id_type=MESH)

    def remote(source, target, send, recv, device):
        return pltpu.make_async_remote_copy(
            src_ref=source, dst_ref=target, send_sem=send, recv_sem=recv,
            device_id=device, device_id_type=MESH,
        )

    def to_peers(source, target, send, recv):
        return [
            remote(source, target, send.at[d], recv.at[d], (b, peer)) for d, peer in enumerate(peers)
        ]

    def there(direction):
        return has_left if direction > 0 else has_right

    def sends(direction):
        return has_right if direction > 0 else has_left

    @pl.when(jnp.logical_not(has_left))
    def _():
        for p in range(g_size):
            buf[p, 0 : 3 * r, :] = jnp.zeros((3 * r, rows), F32)
        near[0] = jnp.zeros(near.shape[1:], F32)
        lin_near[0] = jnp.zeros(lin_near.shape[1:], F32)

    @pl.when(jnp.logical_not(has_right))
    def _():
        for p in range(g_size):
            buf[p, 3 * r : 6 * r, :] = jnp.zeros((3 * r, rows), F32)
        near[1] = jnp.zeros(near.shape[1:], F32)
        lin_near[1] = jnp.zeros(lin_near.shape[1:], F32)

    loads["sketch"].wait()
    order = list(range(1, slots + 1)) + [0]
    flat = jnp.concatenate([sk_v[k] for k in order], axis=0)
    flat_hi, flat_lo = terms(flat, 2)
    flat_both = jnp.concatenate([flat_hi, flat_lo], axis=0)

    piece_copies, own_copies = {}, {}

    def send_piece(block, slot, direction, place):
        here = buf.at[g, pl.ds(place * r, r)]
        if direction == 0:
            buf[g, pl.ds(place * r, r), :] = out_v[block, slot * r : (slot + 1) * r, :]
            own_copies[place] = to_peers(here, here, p1_fsend.at[place], p1_frecv.at[place])
            for copy in own_copies[place]:
                copy.start()
        else:
            copy = remote(
                out_v.at[block, pl.ds(slot * r, r)], here, p1_send.at[place], p1_recv.at[place],
                (b + direction, g),
            )
            piece_copies[place] = (direction, copy)
            pl.when(sends(direction))(copy.start)

    for i in range(blocks):
        loads["inv", i].wait()
        loads["ex", i].wait()
        if i == blocks - 1:
            for name, copy in loads.items():
                if name[0] == "c":
                    copy.start()
        primary = nn(inv_v[i], ex_v[i])
        primary_hi, primary_lo = terms(primary, 2)
        out_v[i] = folded(nt(flat_both, primary_hi), 2) + nt(flat_hi, primary_lo)
        if i == 0:
            neighbours = has_left.astype(jnp.int32) + has_right.astype(jnp.int32)
            pl.semaphore_wait(barrier, g_size - 1 + neighbours)
        for piece in PIECES[:3] if i == 0 else PIECES[3:]:
            send_piece(*piece)

    loads["mask"].wait()
    weights = [[mask_s[i, k].astype(F32) for k in range(slots)] for i in range(blocks)]
    sources = [None] * blocks

    def add_part(place, p):
        i, k = USE[place]
        piece = stacked(buf[p, place * r : (place + 1) * r, :], 3)
        columns = pl.ds(pl.multiple_of(p * rows, rows), rows)
        term = weights[i][k] * folded(nt(piece, c_v[i, k, :, columns]), 3)
        sources[i] = term if sources[i] is None else sources[i] + term

    def add_own(place):
        loads["c", *USE[place]].wait()
        add_part(place, g)

    def add_others(place):
        arrived(place)
        for peer in peers:
            add_part(place, peer)

    def forward(places):
        for place in places:
            direction, copy = piece_copies[place]
            here = buf.at[g, pl.ds(place * r, r)]
            own_copies[place] = to_peers(here, here, p1_fsend.at[place], p1_frecv.at[place])

            @pl.when(there(direction))
            def _():
                copy.wait_recv()
                for out in own_copies[place]:
                    out.start()

    def arrived(place):
        if place in piece_copies:

            @pl.when(there(piece_copies[place][0]))
            def _():
                for out in own_copies[place]:
                    out.wait_recv()
        else:
            for out in own_copies[place]:
                out.wait_recv()

    src_copies, sk_copies, skp_copies, v_copies = {}, {}, {}, {}

    def finish_source(i):
        src[g, i * r : (i + 1) * r, :] = sources[i]
        here = src.at[g, pl.ds(i * r, r)]
        src_copies[i] = to_peers(here, here, src_send.at[i], src_recv.at[i])
        for copy in src_copies[i]:
            copy.start()

    def sketch_block(i):
        for copy in src_copies[i]:
            copy.wait_recv()
        total = None
        for p in range(g_size):
            got = nt(
                stacked(src[p, i * r : (i + 1) * r, :], 3), inv_v[i, :, p * rows : (p + 1) * rows]
            )
            total = got if total is None else total + got
        skt[g, i * r : (i + 1) * r, :] = out_v[i, slots * r : (slots + 1) * r, :] - folded(total, 3)
        here = skt.at[g, pl.ds(i * r, r)]
        for side, direction in enumerate((1, -1)):
            copy = remote(
                here, near.at[side, pl.ds(i * r, r)], sk_send.at[side, i], sk_recv.at[side, i],
                (b + direction, g),
            )
            sk_copies[side, i] = (direction, copy)
            pl.when(sends(direction))(copy.start)
        skp_copies[i] = to_peers(here, here, skp_send.at[i], skp_recv.at[i])
        for copy in skp_copies[i]:
            copy.start()

    def project(i, k):
        got = folded(nn(stacked(skt[g, i * r : (i + 1) * r, :], 3), c_v[i, k]), 3)
        for p in range(g_size):
            v_out[p, (i * slots + k) * r : (i * slots + k + 1) * r, :] = got[:, p * rows : (p + 1) * rows]

    def send_projected(i):
        span = pl.ds(i * slots * r, slots * r)
        v_copies[i] = [
            remote(
                v_out.at[peer, span], v_in.at[d, span], v_send.at[i, d], v_recv.at[i, d], (b, peer)
            )
            for d, peer in enumerate(peers)
        ]
        for copy in v_copies[i]:
            copy.start()

    for place in (7, 6):
        add_own(place)
    for place in (7, 6):
        add_others(place)
    for piece, first in LATER:
        direction, copy = piece_copies[first]
        pl.when(sends(direction))(copy.wait_send)
        send_piece(*piece)
    for place in (0, 4, 2):
        forward((place,))
        add_own(place)
    for place in (0, 4, 2):
        add_others(place)
    finish_source(0)
    forward((3,))
    add_own(3)
    sketch_block(0)
    for place in (1, 5):
        forward((place,))
        add_own(place)
    for place in (3, 1, 5):
        add_others(place)
    finish_source(1)
    for k in range(2):
        project(0, k)
    sketch_block(1)
    for k in range(2, slots):
        project(0, k)
    send_projected(0)
    project(1, 0)

    for i in range(blocks):
        for copy in skp_copies[i]:
            copy.wait_recv()
    grams = []
    for i in range(blocks):
        total = None
        for p in range(g_size):
            part = skt[p, i * r : (i + 1) * r, :]
            got = exact_nt(part, part, 3)
            total = got if total is None else total + got
        grams.append(total * (1.0 / unknowns))
    for k in range(1, slots):
        project(1, k)
    inverses = inverse_factors(grams)
    half = r // 2
    lin[...] = jnp.concatenate(
        [inverse[n : n + half] for inverse in inverses for n in (0, half)], axis=1
    )
    lin_copies = []
    for side, direction in enumerate((1, -1)):
        copy = remote(lin, lin_near.at[side], lin_send.at[side], lin_recv.at[side], (b + direction, g))
        lin_copies.append((direction, copy))
        pl.when(sends(direction))(copy.start)

    send_projected(1)

    wide = slots * r
    row = lax.broadcasted_iota(jnp.int32, (wide, wide), 0) // r
    col = lax.broadcasted_iota(jnp.int32, (wide, wide), 1) // r
    diagonal = row == col

    def wider(x):
        return jnp.concatenate([x] * slots, axis=1)

    def unpacked(x):
        quarters = [x[:, n * r : (n + 1) * r] for n in range(2 * blocks)]
        return [
            wider(jnp.concatenate(quarters[2 * i : 2 * i + 2], axis=0)) for i in range(blocks)
        ]

    projected = []
    for i in range(blocks):
        for copy in v_copies[i]:
            copy.wait_recv()
        span = slice(i * wide, (i + 1) * wide)
        total = v_out[g, pl.ds(i * wide, wide), :]
        for d in range(g_size - 1):
            total = total + v_in[d, span, :]
        factors = jnp.where(diagonal, jnp.concatenate([wider(inverses[i])] * slots, axis=0), 0.0)
        projected.append(exact_nn(factors, total, 3))

    products = {}

    def reduce(users, basis):
        left = [projected[i][k * r : (k + 1) * r] for i, k in users]
        got = exact_nt(left[0] if len(left) == 1 else jnp.concatenate(left, axis=0), basis, 3)
        for n, user in enumerate(users):
            products[user] = got[n * r : (n + 1) * r]

    reduce([(1, 1)], skt[g, 0:r, :])
    reduce([(0, 2)], skt[g, r : 2 * r, :])
    for i, side, users in (
        (0, 0, [(0, 0)]),
        (0, 1, [(0, 3), (1, 2)]),
        (1, 0, [(0, 1), (1, 0)]),
        (1, 1, [(1, 3)]),
    ):
        direction, copy = sk_copies[side, i]
        pl.when(there(direction))(copy.wait_recv)
        reduce(users, near[side, i * r : (i + 1) * r, :])
    for i in range(blocks):
        wbuf[g, i * r : (i + 1) * r, :] = jnp.concatenate([products[i, k] for k in range(slots)], axis=1)
    here = wbuf.at[g]
    w_copies = to_peers(here, here, w_send, w_recv)
    for copy in w_copies:
        copy.start()

    scale = 1.0 / math.sqrt(unknowns)
    for i in range(blocks):
        bases_o[i] = exact_nn(inverses[i], skt[g, i * r : (i + 1) * r, :], 3)
        driven = None
        for p in range(g_size):
            got = nn(stacked(skt[p, i * r : (i + 1) * r, :], 3), ex_v[i, p * rows : (p + 1) * rows, :])
            driven = got if driven is None else driven + got
        re_o[i] = exact_nn(inverses[i], folded(driven, 3), 3) * scale
    for direction, copy in lin_copies:
        pl.when(there(direction))(copy.wait_recv)
    for copy in w_copies:
        copy.wait_recv()
    total = wbuf[0]
    for p in range(1, g_size):
        total = total + wbuf[p]
    (left_a, left_b), (right_a, right_b) = unpacked(lin_near[0]), unpacked(lin_near[1])
    own_a, own_b = [wider(inverse) for inverse in inverses]
    beside = ((left_a, left_b, own_b, right_a), (left_b, own_a, right_a, right_b))
    for i in range(blocks):
        factors = jnp.where(diagonal, jnp.concatenate(beside[i], axis=0), 0.0)
        got = exact_nt(total[i * r : (i + 1) * r], factors, 3) * scale
        for k in range(slots):
            rc_o[i, k] = got[:, k * r : (k + 1) * r]

    waited = [first for _, first in LATER]
    last_pieces = [pair for place, pair in piece_copies.items() if place not in waited]
    for direction, copy in last_pieces + list(sk_copies.values()) + lin_copies:
        pl.when(sends(direction))(copy.wait_send)
    for place, copies in own_copies.items():
        for copy in copies:
            if place in piece_copies:
                pl.when(there(piece_copies[place][0]))(copy.wait_send)
            else:
                copy.wait_send()
    for copies in list(src_copies.values()) + list(skp_copies.values()) + list(v_copies.values()) + [w_copies]:
        for copy in copies:
            copy.wait_send()


def shards(g_size, b_size, excitation, inverse_self, coupling, neighbour_mask, sketch):
    blocks, unknowns, columns = excitation.shape
    rows = inverse_self.shape[1]
    slots = coupling.shape[1]
    sketch = jnp.swapaxes(sketch, 1, 2)
    r = sketch.shape[1]
    assert blocks == 2 and slots == 4 and rows * g_size == unknowns
    others = max(g_size - 1, 1)
    wide = slots * r
    vmem = lambda *shape: pltpu.VMEM(shape, F32)
    dma = lambda *shape: pltpu.SemaphoreType.DMA(shape)
    anywhere = pl.BlockSpec(memory_space=pl.ANY)
    flops = 2 * blocks * rows * unknowns * (columns + 2 * slots * 3 * r)
    bases, reduced, driven = pl.pallas_call(
        functools.partial(kernel, g_size, b_size),
        out_shape=(vmem(blocks, r, rows), vmem(blocks, slots, r, r), vmem(blocks, r, columns)),
        in_specs=[anywhere] * 5,
        out_specs=(pl.BlockSpec(memory_space=pltpu.VMEM),) * 3,
        scratch_shapes=[
            pltpu.VMEM(excitation.shape, BF16),
            pltpu.VMEM(inverse_self.shape, BF16),
            pltpu.VMEM(coupling.shape, BF16),
            vmem(*sketch.shape),
            vmem(blocks, (slots + 1) * r, rows),
            vmem(g_size, 8 * r, rows),
            vmem(g_size, 2 * r, rows),
            vmem(g_size, 2 * r, rows),
            vmem(2, 2 * r, rows),
            vmem(r // 2, 2 * blocks * r),
            vmem(2, r // 2, 2 * blocks * r),
            vmem(g_size, 2 * r, wide),
            vmem(g_size, blocks * wide, rows),
            vmem(others, blocks * wide, rows),
            pltpu.SMEM(neighbour_mask.shape, neighbour_mask.dtype),
            dma(2 + 2 * blocks + blocks * slots),
            dma(6),
            dma(6),
            dma(8, others),
            dma(8, others),
            dma(blocks, others),
            dma(blocks, others),
            dma(2, blocks),
            dma(2, blocks),
            dma(blocks, others),
            dma(blocks, others),
            dma(blocks, others),
            dma(blocks, others),
            dma(2),
            dma(2),
            dma(others),
            dma(others),
        ],
        compiler_params=pltpu.CompilerParams(
            collective_id=0, has_side_effects=True, vmem_limit_bytes=60 * 1024 * 1024
        ),
        cost_estimate=pl.CostEstimate(
            flops=flops, bytes_accessed=2 * (coupling.size + inverse_self.size), transcendentals=0
        ),
        name="basis_currents",
    )(excitation, inverse_self, coupling, neighbour_mask, sketch)
    return jnp.swapaxes(bases, 1, 2), reduced, driven


def solution(mesh):
    return jax.shard_map(
        functools.partial(shards, mesh.shape["grp"], mesh.shape["blk"]),
        mesh=mesh,
        in_specs=(
            P("blk", None, None),
            P("blk", "grp", None),
            P("blk", None, "grp", None),
            P("blk", None),
            P(),
        ),
        out_specs=(P("blk", "grp", None), P("blk", None, None, None), P("blk", None, None)),
        check_vma=False,
    )
```

```python
import functools
import math

import jax
import jax.numpy as jnp
from jax import lax
from jax.experimental import pallas as pl
from jax.experimental.pallas import tpu as pltpu
from jax.sharding import PartitionSpec as P

MESH = pl.DeviceIdType.MESH
F32, BF16 = jnp.float32, jnp.bfloat16

PIECES = (
    (0, 0, 1, 0),
    (0, 3, -1, 4),
    (0, 1, 0, 6),
    (1, 1, 1, 2),
    (1, 2, 0, 7),
)
LATER = (((0, 2, -1, 3), 4), ((1, 0, 1, 1), 0), ((1, 3, -1, 5), 2))
USE = {0: (0, 0), 1: (1, 0), 2: (0, 1), 3: (1, 2), 4: (0, 3), 5: (1, 3), 6: (1, 1), 7: (0, 2)}


def nt(left, right):
    return lax.dot_general(left, right, (((1,), (1,)), ((), ())), preferred_element_type=F32)


def nn(left, right):
    return lax.dot_general(left, right, (((1,), (0,)), ((), ())), preferred_element_type=F32)


def terms(x, count):
    out = []
    for step in range(count):
        part = x.astype(BF16)
        out.append(part)
        if step < count - 1:
            x = x - part.astype(F32)
    return out


def stacked(x, count):
    return jnp.concatenate(terms(x, count), axis=0)


def folded(x, count):
    size = x.shape[0] // count
    total = x[:size]
    for step in range(1, count):
        total = total + x[step * size : (step + 1) * size]
    return total


def exact_nt(left, right, count):
    rows = left.shape[0]
    ls, rs = terms(left, count), terms(right, count)
    total = None
    for order in range(count):
        got = nt(jnp.concatenate(ls[: count - order], axis=0), rs[order])
        got = folded(got, count - order)
        total = got if total is None else total + got
    return total


def exact_nn(left, right, count):
    ls, rs = terms(left, count), terms(right, count)
    total = None
    for order in range(count):
        got = nn(jnp.concatenate(ls[: count - order], axis=0), rs[order])
        got = folded(got, count - order)
        total = got if total is None else total + got
    return total


def inverse_factors(grams):
    size = grams[0].shape[0]
    row = lax.broadcasted_iota(jnp.int32, (size, size), 0)
    col = lax.broadcasted_iota(jnp.int32, (size, size), 1)
    eye = (row == col).astype(F32)
    down = lax.broadcasted_iota(jnp.int32, (size, 1), 0)
    work = [jnp.concatenate([gram, eye], axis=1) for gram in grams]
    width = math.gcd(size, 8)
    for first in range(0, size, width):
        span = range(first, first + width)
        for n, a in enumerate(work):
            columns = {k: jnp.broadcast_to(a[:, k : k + 1], a.shape) for k in span}
            lines = {k: a[k : k + 1, :] for k in span}
            for k in span:
                factor = 1.0 / columns[k][k : k + 1, :]
                line = lines[k] * factor
                lead = jnp.where(down > k, columns[k], 0.0)
                for t in range(k + 1, first + width):
                    lines[t] = lines[t] - columns[k][t : t + 1, :] * line
                    columns[t] = columns[t] - lead * (columns[t][k : k + 1, :] * factor)
                a = a - lead * line
            work[n] = a
    out = []
    for a in work:
        diag = jnp.sum(jnp.where(row == col, a[:, :size], 0.0), axis=1, keepdims=True)
        out.append(a[:, size:] / jnp.sqrt(diag))
    return out


def kernel(
    g_size, b_size, ex, inv, coup, mask, sketch, bases_o, rc_o, re_o,
    ex_v, inv_v, c_v, sk_v, out_v, buf, src, skt, near, lin, lin_near, wbuf, v_out, v_in, mask_s,
    load_sem, p1_send, p1_recv, p1_fsend, p1_frecv, src_send, src_recv,
    sk_send, sk_recv, skp_send, skp_recv, v_send, v_recv, lin_send, lin_recv, w_send, w_recv,
):
    b, g = lax.axis_index("blk"), lax.axis_index("grp")
    has_left, has_right = b > 0, b < b_size - 1
    blocks, unknowns, _ = ex.shape
    rows = inv.shape[1]
    slots = coup.shape[1]
    r = sketch.shape[1]
    peers = [lax.rem(g + d, g_size) for d in range(1, g_size)]

    def load(number, source, target):
        return pltpu.make_async_copy(source, target, load_sem.at[number])

    loads = {}
    loads["sketch"] = load(0, sketch, sk_v)
    loads["mask"] = load(1 + 2 * blocks + blocks * slots, mask, mask_s)
    for i in range(blocks):
        loads["inv", i] = load(1 + 2 * i, inv.at[i], inv_v.at[i])
        loads["ex", i] = load(2 + 2 * i, ex.at[i], ex_v.at[i])
    for number, place in enumerate((7, 6, 0, 4, 2, 3, 1, 5)):
        i, k = USE[place]
        loads["c", i, k] = load(1 + 2 * blocks + number, coup.at[i, k], c_v.at[i, k])
    for name, copy in loads.items():
        if name[0] != "c":
            copy.start()

    barrier = pltpu.get_barrier_semaphore()

    @pl.when(has_left)
    def _():
        pl.semaphore_signal(barrier, inc=1, device_id=(b - 1, g), device_id_type=MESH)

    @pl.when(has_right)
    def _():
        pl.semaphore_signal(barrier, inc=1, device_id=(b + 1, g), device_id_type=MESH)

    for peer in peers:
        pl.semaphore_signal(barrier, inc=1, device_id=(b, peer), device_id_type=MESH)

    def remote(source, target, send, recv, device):
        return pltpu.make_async_remote_copy(
            src_ref=source, dst_ref=target, send_sem=send, recv_sem=recv,
            device_id=device, device_id_type=MESH,
        )

    def to_peers(source, target, send, recv):
        return [
            remote(source, target, send.at[d], recv.at[d], (b, peer)) for d, peer in enumerate(peers)
        ]

    def there(direction):
        return has_left if direction > 0 else has_right

    def sends(direction):
        return has_right if direction > 0 else has_left

    @pl.when(jnp.logical_not(has_left))
    def _():
        for p in range(g_size):
            buf[p, 0 : 3 * r, :] = jnp.zeros((3 * r, rows), F32)
        near[0] = jnp.zeros(near.shape[1:], F32)
        lin_near[0] = jnp.zeros(lin_near.shape[1:], F32)

    @pl.when(jnp.logical_not(has_right))
    def _():
        for p in range(g_size):
            buf[p, 3 * r : 6 * r, :] = jnp.zeros((3 * r, rows), F32)
        near[1] = jnp.zeros(near.shape[1:], F32)
        lin_near[1] = jnp.zeros(lin_near.shape[1:], F32)

    loads["sketch"].wait()
    order = list(range(1, slots + 1)) + [0]
    flat = jnp.concatenate([sk_v[k] for k in order], axis=0)
    flat_hi, flat_lo = terms(flat, 2)
    flat_both = jnp.concatenate([flat_hi, flat_lo], axis=0)

    piece_copies, own_copies = {}, {}

    def send_piece(block, slot, direction, place):
        here = buf.at[g, pl.ds(place * r, r)]
        if direction == 0:
            buf[g, pl.ds(place * r, r), :] = out_v[block, slot * r : (slot + 1) * r, :]
            own_copies[place] = to_peers(here, here, p1_fsend.at[place], p1_frecv.at[place])
            for copy in own_copies[place]:
                copy.start()
        else:
            copy = remote(
                out_v.at[block, pl.ds(slot * r, r)], here, p1_send.at[place], p1_recv.at[place],
                (b + direction, g),
            )
            piece_copies[place] = (direction, copy)
            pl.when(sends(direction))(copy.start)

    for i in range(blocks):
        loads["inv", i].wait()
        loads["ex", i].wait()
        if i == blocks - 1:
            for name, copy in loads.items():
                if name[0] == "c":
                    copy.start()
        primary = nn(inv_v[i], ex_v[i])
        primary_hi, primary_lo = terms(primary, 2)
        out_v[i] = folded(nt(flat_both, primary_hi), 2) + nt(flat_hi, primary_lo)
        if i == 0:
            neighbours = has_left.astype(jnp.int32) + has_right.astype(jnp.int32)
            pl.semaphore_wait(barrier, g_size - 1 + neighbours)
        for piece in PIECES[:3] if i == 0 else PIECES[3:]:
            send_piece(*piece)

    loads["mask"].wait()
    weights = [[mask_s[i, k].astype(F32) for k in range(slots)] for i in range(blocks)]
    sources = [None] * blocks

    def add_part(place, p):
        i, k = USE[place]
        piece = stacked(buf[p, place * r : (place + 1) * r, :], 3)
        columns = pl.ds(pl.multiple_of(p * rows, rows), rows)
        term = weights[i][k] * folded(nt(piece, c_v[i, k, :, columns]), 3)
        sources[i] = term if sources[i] is None else sources[i] + term

    def add_own(place):
        loads["c", *USE[place]].wait()
        add_part(place, g)

    def add_others(place):
        arrived(place)
        for peer in peers:
            add_part(place, peer)

    def forward(places):
        for place in places:
            direction, copy = piece_copies[place]
            here = buf.at[g, pl.ds(place * r, r)]
            own_copies[place] = to_peers(here, here, p1_fsend.at[place], p1_frecv.at[place])

            @pl.when(there(direction))
            def _():
                copy.wait_recv()
                for out in own_copies[place]:
                    out.start()

    def arrived(place):
        if place in piece_copies:

            @pl.when(there(piece_copies[place][0]))
            def _():
                for out in own_copies[place]:
                    out.wait_recv()
        else:
            for out in own_copies[place]:
                out.wait_recv()

    src_copies, sk_copies, skp_copies, v_copies = {}, {}, {}, {}

    def finish_source(i):
        src[g, i * r : (i + 1) * r, :] = sources[i]
        here = src.at[g, pl.ds(i * r, r)]
        src_copies[i] = to_peers(here, here, src_send.at[i], src_recv.at[i])
        for copy in src_copies[i]:
            copy.start()

    def sketch_block(i):
        for copy in src_copies[i]:
            copy.wait_recv()
        total = None
        for p in range(g_size):
            got = nt(
                stacked(src[p, i * r : (i + 1) * r, :], 3), inv_v[i, :, p * rows : (p + 1) * rows]
            )
            total = got if total is None else total + got
        skt[g, i * r : (i + 1) * r, :] = out_v[i, slots * r : (slots + 1) * r, :] - folded(total, 3)
        here = skt.at[g, pl.ds(i * r, r)]
        for side, direction in enumerate((1, -1)):
            copy = remote(
                here, near.at[side, pl.ds(i * r, r)], sk_send.at[side, i], sk_recv.at[side, i],
                (b + direction, g),
            )
            sk_copies[side, i] = (direction, copy)
            pl.when(sends(direction))(copy.start)
        skp_copies[i] = to_peers(here, here, skp_send.at[i], skp_recv.at[i])
        for copy in skp_copies[i]:
            copy.start()

    def project(i, k):
        got = folded(nn(stacked(skt[g, i * r : (i + 1) * r, :], 3), c_v[i, k]), 3)
        for p in range(g_size):
            v_out[p, (i * slots + k) * r : (i * slots + k + 1) * r, :] = got[:, p * rows : (p + 1) * rows]

    def send_projected(i):
        span = pl.ds(i * slots * r, slots * r)
        v_copies[i] = [
            remote(
                v_out.at[peer, span], v_in.at[d, span], v_send.at[i, d], v_recv.at[i, d], (b, peer)
            )
            for d, peer in enumerate(peers)
        ]
        for copy in v_copies[i]:
            copy.start()

    for place in (7, 6):
        add_own(place)
    for place in (7, 6):
        add_others(place)
    for piece, first in LATER:
        direction, copy = piece_copies[first]
        pl.when(sends(direction))(copy.wait_send)
        send_piece(*piece)
    for place in (0, 4, 2):
        forward((place,))
        add_own(place)
    for place in (0, 4, 2):
        add_others(place)
    finish_source(0)
    forward((3,))
    add_own(3)
    sketch_block(0)
    for k in range(2):
        project(0, k)
    for place in (1, 5):
        forward((place,))
        add_own(place)
    for place in (3, 1, 5):
        add_others(place)
    finish_source(1)
    for k in range(2, slots):
        project(0, k)
    send_projected(0)
    sketch_block(1)
    for k in range(slots):
        project(1, k)
    send_projected(1)

    for i in range(blocks):
        for copy in skp_copies[i]:
            copy.wait_recv()
    grams = []
    for i in range(blocks):
        total = None
        for p in range(g_size):
            part = skt[p, i * r : (i + 1) * r, :]
            got = exact_nt(part, part, 3)
            total = got if total is None else total + got
        grams.append(total * (1.0 / unknowns))
    inverses = inverse_factors(grams)
    half = r // 2
    lin[...] = jnp.concatenate(
        [inverse[n : n + half] for inverse in inverses for n in (0, half)], axis=1
    )
    lin_copies = []
    for side, direction in enumerate((1, -1)):
        copy = remote(lin, lin_near.at[side], lin_send.at[side], lin_recv.at[side], (b + direction, g))
        lin_copies.append((direction, copy))
        pl.when(sends(direction))(copy.start)

    wide = slots * r
    row = lax.broadcasted_iota(jnp.int32, (wide, wide), 0) // r
    col = lax.broadcasted_iota(jnp.int32, (wide, wide), 1) // r
    diagonal = row == col

    def wider(x):
        return jnp.concatenate([x] * slots, axis=1)

    def unpacked(x):
        quarters = [x[:, n * r : (n + 1) * r] for n in range(2 * blocks)]
        return [
            wider(jnp.concatenate(quarters[2 * i : 2 * i + 2], axis=0)) for i in range(blocks)
        ]

    projected = []
    for i in range(blocks):
        for copy in v_copies[i]:
            copy.wait_recv()
        span = slice(i * wide, (i + 1) * wide)
        total = v_out[g, pl.ds(i * wide, wide), :]
        for d in range(g_size - 1):
            total = total + v_in[d, span, :]
        factors = jnp.where(diagonal, jnp.concatenate([wider(inverses[i])] * slots, axis=0), 0.0)
        projected.append(exact_nn(factors, total, 3))

    products = {}

    def reduce(users, basis):
        left = [projected[i][k * r : (k + 1) * r] for i, k in users]
        got = exact_nt(left[0] if len(left) == 1 else jnp.concatenate(left, axis=0), basis, 3)
        for n, user in enumerate(users):
            products[user] = got[n * r : (n + 1) * r]

    reduce([(1, 1)], skt[g, 0:r, :])
    reduce([(0, 2)], skt[g, r : 2 * r, :])
    for i, side, users in (
        (0, 0, [(0, 0)]),
        (0, 1, [(0, 3), (1, 2)]),
        (1, 0, [(0, 1), (1, 0)]),
        (1, 1, [(1, 3)]),
    ):
        direction, copy = sk_copies[side, i]
        pl.when(there(direction))(copy.wait_recv)
        reduce(users, near[side, i * r : (i + 1) * r, :])
    for i in range(blocks):
        wbuf[g, i * r : (i + 1) * r, :] = jnp.concatenate([products[i, k] for k in range(slots)], axis=1)
    here = wbuf.at[g]
    w_copies = to_peers(here, here, w_send, w_recv)
    for copy in w_copies:
        copy.start()

    scale = 1.0 / math.sqrt(unknowns)
    for i in range(blocks):
        bases_o[i] = exact_nn(inverses[i], skt[g, i * r : (i + 1) * r, :], 3)
        driven = None
        for p in range(g_size):
            got = nn(stacked(skt[p, i * r : (i + 1) * r, :], 3), ex_v[i, p * rows : (p + 1) * rows, :])
            driven = got if driven is None else driven + got
        re_o[i] = exact_nn(inverses[i], folded(driven, 3), 3) * scale
    for direction, copy in lin_copies:
        pl.when(there(direction))(copy.wait_recv)
    for copy in w_copies:
        copy.wait_recv()
    total = wbuf[0]
    for p in range(1, g_size):
        total = total + wbuf[p]
    (left_a, left_b), (right_a, right_b) = unpacked(lin_near[0]), unpacked(lin_near[1])
    own_a, own_b = [wider(inverse) for inverse in inverses]
    beside = ((left_a, left_b, own_b, right_a), (left_b, own_a, right_a, right_b))
    for i in range(blocks):
        factors = jnp.where(diagonal, jnp.concatenate(beside[i], axis=0), 0.0)
        got = exact_nt(total[i * r : (i + 1) * r], factors, 3) * scale
        for k in range(slots):
            rc_o[i, k] = got[:, k * r : (k + 1) * r]

    waited = [first for _, first in LATER]
    last_pieces = [pair for place, pair in piece_copies.items() if place not in waited]
    for direction, copy in last_pieces + list(sk_copies.values()) + lin_copies:
        pl.when(sends(direction))(copy.wait_send)
    for place, copies in own_copies.items():
        for copy in copies:
            if place in piece_copies:
                pl.when(there(piece_copies[place][0]))(copy.wait_send)
            else:
                copy.wait_send()
    for copies in list(src_copies.values()) + list(skp_copies.values()) + list(v_copies.values()) + [w_copies]:
        for copy in copies:
            copy.wait_send()


def hand_over(a, b, c, a_out, b_out, c_out, sems):
    copies = [
        pltpu.make_async_copy(source, target, sems.at[n])
        for n, (source, target) in enumerate(((a, a_out), (b, b_out), (c, c_out)))
    ]
    for copy in copies:
        copy.start()
    for copy in copies:
        copy.wait()


def shards(g_size, b_size, excitation, inverse_self, coupling, neighbour_mask, sketch):
    blocks, unknowns, columns = excitation.shape
    rows = inverse_self.shape[1]
    slots = coupling.shape[1]
    sketch = jnp.swapaxes(sketch, 1, 2)
    r = sketch.shape[1]
    assert blocks == 2 and slots == 4 and rows * g_size == unknowns
    others = max(g_size - 1, 1)
    wide = slots * r
    vmem = lambda *shape: pltpu.VMEM(shape, F32)
    dma = lambda *shape: pltpu.SemaphoreType.DMA(shape)
    anywhere = pl.BlockSpec(memory_space=pl.ANY)
    flops = 2 * blocks * rows * unknowns * (columns + 2 * slots * 3 * r)
    bases, reduced, driven = pl.pallas_call(
        functools.partial(kernel, g_size, b_size),
        out_shape=(vmem(blocks, r, rows), vmem(blocks, slots, r, r), vmem(blocks, r, columns)),
        in_specs=[anywhere] * 5,
        out_specs=(pl.BlockSpec(memory_space=pltpu.VMEM),) * 3,
        scratch_shapes=[
            pltpu.VMEM(excitation.shape, BF16),
            pltpu.VMEM(inverse_self.shape, BF16),
            pltpu.VMEM(coupling.shape, BF16),
            vmem(*sketch.shape),
            vmem(blocks, (slots + 1) * r, rows),
            vmem(g_size, 8 * r, rows),
            vmem(g_size, 2 * r, rows),
            vmem(g_size, 2 * r, rows),
            vmem(2, 2 * r, rows),
            vmem(r // 2, 2 * blocks * r),
            vmem(2, r // 2, 2 * blocks * r),
            vmem(g_size, 2 * r, wide),
            vmem(g_size, blocks * wide, rows),
            vmem(others, blocks * wide, rows),
            pltpu.SMEM(neighbour_mask.shape, neighbour_mask.dtype),
            dma(2 + 2 * blocks + blocks * slots),
            dma(6),
            dma(6),
            dma(8, others),
            dma(8, others),
            dma(blocks, others),
            dma(blocks, others),
            dma(2, blocks),
            dma(2, blocks),
            dma(blocks, others),
            dma(blocks, others),
            dma(blocks, others),
            dma(blocks, others),
            dma(2),
            dma(2),
            dma(others),
            dma(others),
        ],
        compiler_params=pltpu.CompilerParams(
            collective_id=0, has_side_effects=True, vmem_limit_bytes=60 * 1024 * 1024
        ),
        cost_estimate=pl.CostEstimate(
            flops=flops, bytes_accessed=2 * (coupling.size + inverse_self.size), transcendentals=0
        ),
        name="basis_currents",
    )(excitation, inverse_self, coupling, neighbour_mask, sketch)
    results = (bases, reduced, driven)
    bases, reduced, driven = pl.pallas_call(
        hand_over,
        out_shape=tuple(jax.ShapeDtypeStruct(x.shape, x.dtype) for x in results),
        in_specs=[pl.BlockSpec(memory_space=pltpu.VMEM)] * 3,
        out_specs=(anywhere,) * 3,
        scratch_shapes=[dma(3)],
        name="hand_over",
    )(*results)
    return jnp.swapaxes(bases, 1, 2), reduced, driven


def solution(mesh):
    return jax.shard_map(
        functools.partial(shards, mesh.shape["grp"], mesh.shape["blk"]),
        mesh=mesh,
        in_specs=(
            P("blk", None, None),
            P("blk", "grp", None),
            P("blk", None, "grp", None),
            P("blk", None),
            P(),
        ),
        out_specs=(P("blk", "grp", None), P("blk", None, None, None), P("blk", None, None)),
        check_vma=False,
    )
```

```python
import functools
import math

import jax
import jax.numpy as jnp
from jax import lax
from jax.experimental import pallas as pl
from jax.experimental.pallas import tpu as pltpu
from jax.sharding import PartitionSpec as P

MESH = pl.DeviceIdType.MESH
F32, BF16 = jnp.float32, jnp.bfloat16

PIECES = (
    (0, 0, 1, 0),
    (0, 3, -1, 4),
    (0, 1, 0, 6),
    (1, 1, 1, 2),
    (1, 2, 0, 7),
    (0, 2, -1, 3),
    (1, 0, 1, 1),
    (1, 3, -1, 5),
)
USE = {0: (0, 0), 1: (1, 0), 2: (0, 1), 3: (1, 2), 4: (0, 3), 5: (1, 3), 6: (1, 1), 7: (0, 2)}


def nt(left, right):
    return lax.dot_general(left, right, (((1,), (1,)), ((), ())), preferred_element_type=F32)


def nn(left, right):
    return lax.dot_general(left, right, (((1,), (0,)), ((), ())), preferred_element_type=F32)


def terms(x, count):
    out = []
    for step in range(count):
        part = x.astype(BF16)
        out.append(part)
        if step < count - 1:
            x = x - part.astype(F32)
    return out


def stacked(x, count):
    return jnp.concatenate(terms(x, count), axis=0)


def folded(x, count):
    size = x.shape[0] // count
    total = x[:size]
    for step in range(1, count):
        total = total + x[step * size : (step + 1) * size]
    return total


def exact_nt(left, right, count):
    rows = left.shape[0]
    ls, rs = terms(left, count), terms(right, count)
    total = None
    for order in range(count):
        got = nt(jnp.concatenate(ls[: count - order], axis=0), rs[order])
        got = folded(got, count - order)
        total = got if total is None else total + got
    return total


def exact_nn(left, right, count):
    ls, rs = terms(left, count), terms(right, count)
    total = None
    for order in range(count):
        got = nn(jnp.concatenate(ls[: count - order], axis=0), rs[order])
        got = folded(got, count - order)
        total = got if total is None else total + got
    return total


def inverse_factors(grams):
    size = grams[0].shape[0]
    row = lax.broadcasted_iota(jnp.int32, (size, size), 0)
    col = lax.broadcasted_iota(jnp.int32, (size, size), 1)
    eye = (row == col).astype(F32)
    down = lax.broadcasted_iota(jnp.int32, (size, 1), 0)
    work = [jnp.concatenate([gram, eye], axis=1) for gram in grams]
    width = math.gcd(size, 8)
    for first in range(0, size, width):
        span = range(first, first + width)
        for n, a in enumerate(work):
            columns = {k: jnp.broadcast_to(a[:, k : k + 1], a.shape) for k in span}
            lines = {k: a[k : k + 1, :] for k in span}
            for k in span:
                factor = 1.0 / columns[k][k : k + 1, :]
                line = lines[k] * factor
                lead = jnp.where(down > k, columns[k], 0.0)
                for t in range(k + 1, first + width):
                    lines[t] = lines[t] - columns[k][t : t + 1, :] * line
                    columns[t] = columns[t] - lead * (columns[t][k : k + 1, :] * factor)
                a = a - lead * line
            work[n] = a
    out = []
    for a in work:
        diag = jnp.sum(jnp.where(row == col, a[:, :size], 0.0), axis=1, keepdims=True)
        out.append(a[:, size:] / jnp.sqrt(diag))
    return out


def kernel(
    g_size, b_size, ex, inv, coup, mask, sketch, bases_o, rc_o, re_o,
    ex_v, inv_v, c_v, sk_v, out_v, buf, src, skt, near, lin, lin_near, wbuf, v_out, v_in, mask_s,
    load_sem, p1_send, p1_recv, p1_fsend, p1_frecv, src_send, src_recv,
    sk_send, sk_recv, skp_send, skp_recv, v_send, v_recv, lin_send, lin_recv, w_send, w_recv,
):
    b, g = lax.axis_index("blk"), lax.axis_index("grp")
    has_left, has_right = b > 0, b < b_size - 1
    blocks, unknowns, _ = ex.shape
    rows = inv.shape[1]
    slots = coup.shape[1]
    r = sketch.shape[1]
    peers = [lax.rem(g + d, g_size) for d in range(1, g_size)]

    def load(number, source, target):
        return pltpu.make_async_copy(source, target, load_sem.at[number])

    loads = {}
    loads["sketch"] = load(0, sketch, sk_v)
    loads["mask"] = load(1 + 2 * blocks + blocks * slots, mask, mask_s)
    for i in range(blocks):
        loads["inv", i] = load(1 + 2 * i, inv.at[i], inv_v.at[i])
        loads["ex", i] = load(2 + 2 * i, ex.at[i], ex_v.at[i])
    for number, place in enumerate((7, 6, 0, 4, 2, 3, 1, 5)):
        i, k = USE[place]
        loads["c", i, k] = load(1 + 2 * blocks + number, coup.at[i, k], c_v.at[i, k])
    for name, copy in loads.items():
        if name[0] != "c":
            copy.start()

    barrier = pltpu.get_barrier_semaphore()

    @pl.when(has_left)
    def _():
        pl.semaphore_signal(barrier, inc=1, device_id=(b - 1, g), device_id_type=MESH)

    @pl.when(has_right)
    def _():
        pl.semaphore_signal(barrier, inc=1, device_id=(b + 1, g), device_id_type=MESH)

    for peer in peers:
        pl.semaphore_signal(barrier, inc=1, device_id=(b, peer), device_id_type=MESH)

    def remote(source, target, send, recv, device):
        return pltpu.make_async_remote_copy(
            src_ref=source, dst_ref=target, send_sem=send, recv_sem=recv,
            device_id=device, device_id_type=MESH,
        )

    def to_peers(source, target, send, recv):
        return [
            remote(source, target, send.at[d], recv.at[d], (b, peer)) for d, peer in enumerate(peers)
        ]

    def there(direction):
        return has_left if direction > 0 else has_right

    def sends(direction):
        return has_right if direction > 0 else has_left

    @pl.when(jnp.logical_not(has_left))
    def _():
        for p in range(g_size):
            buf[p, 0 : 3 * r, :] = jnp.zeros((3 * r, rows), F32)
        near[0] = jnp.zeros(near.shape[1:], F32)
        lin_near[0] = jnp.zeros(lin_near.shape[1:], F32)

    @pl.when(jnp.logical_not(has_right))
    def _():
        for p in range(g_size):
            buf[p, 3 * r : 6 * r, :] = jnp.zeros((3 * r, rows), F32)
        near[1] = jnp.zeros(near.shape[1:], F32)
        lin_near[1] = jnp.zeros(lin_near.shape[1:], F32)

    loads["sketch"].wait()
    order = list(range(1, slots + 1)) + [0]
    flat = jnp.concatenate([sk_v[k] for k in order], axis=0)
    flat_hi, flat_lo = terms(flat, 2)
    flat_both = jnp.concatenate([flat_hi, flat_lo], axis=0)

    piece_copies, own_copies = {}, {}

    def send_piece(block, slot, direction, place):
        here = buf.at[g, pl.ds(place * r, r)]
        if direction == 0:
            buf[g, pl.ds(place * r, r), :] = out_v[block, slot * r : (slot + 1) * r, :]
            own_copies[place] = to_peers(here, here, p1_fsend.at[place], p1_frecv.at[place])
            for copy in own_copies[place]:
                copy.start()
        else:
            copy = remote(
                out_v.at[block, pl.ds(slot * r, r)], here, p1_send.at[place], p1_recv.at[place],
                (b + direction, g),
            )
            piece_copies[place] = (direction, copy)
            pl.when(sends(direction))(copy.start)

    for i in range(blocks):
        loads["inv", i].wait()
        loads["ex", i].wait()
        if i == blocks - 1:
            for name, copy in loads.items():
                if name[0] == "c":
                    copy.start()
        primary = nn(inv_v[i], ex_v[i])
        primary_hi, primary_lo = terms(primary, 2)
        out_v[i] = folded(nt(flat_both, primary_hi), 2) + nt(flat_hi, primary_lo)
        if i == 0:
            neighbours = has_left.astype(jnp.int32) + has_right.astype(jnp.int32)
            pl.semaphore_wait(barrier, g_size - 1 + neighbours)
        for piece in PIECES[:3] if i == 0 else PIECES[3:]:
            send_piece(*piece)

    loads["mask"].wait()
    weights = [[mask_s[i, k].astype(F32) for k in range(slots)] for i in range(blocks)]
    sources = [None] * blocks

    def add_part(place, p):
        i, k = USE[place]
        piece = stacked(buf[p, place * r : (place + 1) * r, :], 3)
        columns = pl.ds(pl.multiple_of(p * rows, rows), rows)
        term = weights[i][k] * folded(nt(piece, c_v[i, k, :, columns]), 3)
        sources[i] = term if sources[i] is None else sources[i] + term

    def add_own(place):
        loads["c", *USE[place]].wait()
        add_part(place, g)

    def add_others(place):
        arrived(place)
        for peer in peers:
            add_part(place, peer)

    def forward(places):
        for place in places:
            direction, copy = piece_copies[place]
            here = buf.at[g, pl.ds(place * r, r)]
            own_copies[place] = to_peers(here, here, p1_fsend.at[place], p1_frecv.at[place])

            @pl.when(there(direction))
            def _():
                copy.wait_recv()
                for out in own_copies[place]:
                    out.start()

    def arrived(place):
        if place in piece_copies:

            @pl.when(there(piece_copies[place][0]))
            def _():
                for out in own_copies[place]:
                    out.wait_recv()
        else:
            for out in own_copies[place]:
                out.wait_recv()

    src_copies, sk_copies, skp_copies, v_copies = {}, {}, {}, {}

    def finish_source(i):
        src[g, i * r : (i + 1) * r, :] = sources[i]
        here = src.at[g, pl.ds(i * r, r)]
        src_copies[i] = to_peers(here, here, src_send.at[i], src_recv.at[i])
        for copy in src_copies[i]:
            copy.start()

    def sketch_block(i):
        for copy in src_copies[i]:
            copy.wait_recv()
        total = None
        for p in range(g_size):
            got = nt(
                stacked(src[p, i * r : (i + 1) * r, :], 3), inv_v[i, :, p * rows : (p + 1) * rows]
            )
            total = got if total is None else total + got
        skt[g, i * r : (i + 1) * r, :] = out_v[i, slots * r : (slots + 1) * r, :] - folded(total, 3)
        here = skt.at[g, pl.ds(i * r, r)]
        for side, direction in enumerate((1, -1)):
            copy = remote(
                here, near.at[side, pl.ds(i * r, r)], sk_send.at[side, i], sk_recv.at[side, i],
                (b + direction, g),
            )
            sk_copies[side, i] = (direction, copy)
            pl.when(sends(direction))(copy.start)
        skp_copies[i] = to_peers(here, here, skp_send.at[i], skp_recv.at[i])
        for copy in skp_copies[i]:
            copy.start()

    def project(i, k):
        got = folded(nn(stacked(skt[g, i * r : (i + 1) * r, :], 3), c_v[i, k]), 3)
        for p in range(g_size):
            v_out[p, (i * slots + k) * r : (i * slots + k + 1) * r, :] = got[:, p * rows : (p + 1) * rows]

    def send_projected(i):
        span = pl.ds(i * slots * r, slots * r)
        v_copies[i] = [
            remote(
                v_out.at[peer, span], v_in.at[d, span], v_send.at[i, d], v_recv.at[i, d], (b, peer)
            )
            for d, peer in enumerate(peers)
        ]
        for copy in v_copies[i]:
            copy.start()

    for place in (7, 6):
        add_own(place)
    for place in (7, 6):
        add_others(place)
    for place in (0, 4, 2):
        forward((place,))
        add_own(place)
    for place in (0, 4, 2):
        add_others(place)
    finish_source(0)
    forward((3,))
    add_own(3)
    sketch_block(0)
    for place in (1, 5):
        forward((place,))
        add_own(place)
    for place in (3, 1, 5):
        add_others(place)
    finish_source(1)
    for k in range(2):
        project(0, k)
    sketch_block(1)
    for k in range(2, slots):
        project(0, k)
    send_projected(0)
    project(1, 0)

    for i in range(blocks):
        for copy in skp_copies[i]:
            copy.wait_recv()
    grams = []
    for i in range(blocks):
        total = None
        for p in range(g_size):
            part = skt[p, i * r : (i + 1) * r, :]
            got = exact_nt(part, part, 3)
            total = got if total is None else total + got
        grams.append(total * (1.0 / unknowns))
    for k in range(1, slots):
        project(1, k)
    inverses = inverse_factors(grams)
    half = r // 2
    lin[...] = jnp.concatenate(
        [inverse[n : n + half] for inverse in inverses for n in (0, half)], axis=1
    )
    lin_copies = []
    for side, direction in enumerate((1, -1)):
        copy = remote(lin, lin_near.at[side], lin_send.at[side], lin_recv.at[side], (b + direction, g))
        lin_copies.append((direction, copy))
        pl.when(sends(direction))(copy.start)

    send_projected(1)

    wide = slots * r
    row = lax.broadcasted_iota(jnp.int32, (wide, wide), 0) // r
    col = lax.broadcasted_iota(jnp.int32, (wide, wide), 1) // r
    diagonal = row == col

    def wider(x):
        return jnp.concatenate([x] * slots, axis=1)

    def unpacked(x):
        quarters = [x[:, n * r : (n + 1) * r] for n in range(2 * blocks)]
        return [
            wider(jnp.concatenate(quarters[2 * i : 2 * i + 2], axis=0)) for i in range(blocks)
        ]

    projected = []
    for i in range(blocks):
        for copy in v_copies[i]:
            copy.wait_recv()
        span = slice(i * wide, (i + 1) * wide)
        total = v_out[g, pl.ds(i * wide, wide), :]
        for d in range(g_size - 1):
            total = total + v_in[d, span, :]
        factors = jnp.where(diagonal, jnp.concatenate([wider(inverses[i])] * slots, axis=0), 0.0)
        projected.append(exact_nn(factors, total, 3))

    products = {}

    def reduce(users, basis):
        left = [projected[i][k * r : (k + 1) * r] for i, k in users]
        got = exact_nt(left[0] if len(left) == 1 else jnp.concatenate(left, axis=0), basis, 3)
        for n, user in enumerate(users):
            products[user] = got[n * r : (n + 1) * r]

    reduce([(1, 1)], skt[g, 0:r, :])
    reduce([(0, 2)], skt[g, r : 2 * r, :])
    for i, side, users in (
        (0, 0, [(0, 0)]),
        (0, 1, [(0, 3), (1, 2)]),
        (1, 0, [(0, 1), (1, 0)]),
        (1, 1, [(1, 3)]),
    ):
        direction, copy = sk_copies[side, i]
        pl.when(there(direction))(copy.wait_recv)
        reduce(users, near[side, i * r : (i + 1) * r, :])
    for i in range(blocks):
        wbuf[g, i * r : (i + 1) * r, :] = jnp.concatenate([products[i, k] for k in range(slots)], axis=1)
    here = wbuf.at[g]
    w_copies = to_peers(here, here, w_send, w_recv)
    for copy in w_copies:
        copy.start()

    scale = 1.0 / math.sqrt(unknowns)
    for i in range(blocks):
        bases_o[i] = exact_nn(inverses[i], skt[g, i * r : (i + 1) * r, :], 3)
        driven = None
        for p in range(g_size):
            got = nn(stacked(skt[p, i * r : (i + 1) * r, :], 3), ex_v[i, p * rows : (p + 1) * rows, :])
            driven = got if driven is None else driven + got
        re_o[i] = exact_nn(inverses[i], folded(driven, 3), 3) * scale
    for direction, copy in lin_copies:
        pl.when(there(direction))(copy.wait_recv)
    for copy in w_copies:
        copy.wait_recv()
    total = wbuf[0]
    for p in range(1, g_size):
        total = total + wbuf[p]
    (left_a, left_b), (right_a, right_b) = unpacked(lin_near[0]), unpacked(lin_near[1])
    own_a, own_b = [wider(inverse) for inverse in inverses]
    beside = ((left_a, left_b, own_b, right_a), (left_b, own_a, right_a, right_b))
    for i in range(blocks):
        factors = jnp.where(diagonal, jnp.concatenate(beside[i], axis=0), 0.0)
        got = exact_nt(total[i * r : (i + 1) * r], factors, 3) * scale
        for k in range(slots):
            rc_o[i, k] = got[:, k * r : (k + 1) * r]

    for direction, copy in list(piece_copies.values()) + list(sk_copies.values()) + lin_copies:
        pl.when(sends(direction))(copy.wait_send)
    for place, copies in own_copies.items():
        for copy in copies:
            if place in piece_copies:
                pl.when(there(piece_copies[place][0]))(copy.wait_send)
            else:
                copy.wait_send()
    for copies in list(src_copies.values()) + list(skp_copies.values()) + list(v_copies.values()) + [w_copies]:
        for copy in copies:
            copy.wait_send()


def shards(g_size, b_size, excitation, inverse_self, coupling, neighbour_mask, sketch):
    blocks, unknowns, columns = excitation.shape
    rows = inverse_self.shape[1]
    slots = coupling.shape[1]
    sketch = jnp.swapaxes(sketch, 1, 2)
    r = sketch.shape[1]
    assert blocks == 2 and slots == 4 and rows * g_size == unknowns
    others = max(g_size - 1, 1)
    wide = slots * r
    vmem = lambda *shape: pltpu.VMEM(shape, F32)
    dma = lambda *shape: pltpu.SemaphoreType.DMA(shape)
    anywhere = pl.BlockSpec(memory_space=pl.ANY)
    flops = 2 * blocks * rows * unknowns * (columns + 2 * slots * 3 * r)
    bases, reduced, driven = pl.pallas_call(
        functools.partial(kernel, g_size, b_size),
        out_shape=(vmem(blocks, r, rows), vmem(blocks, slots, r, r), vmem(blocks, r, columns)),
        in_specs=[anywhere] * 5,
        out_specs=(pl.BlockSpec(memory_space=pltpu.VMEM),) * 3,
        scratch_shapes=[
            pltpu.VMEM(excitation.shape, BF16),
            pltpu.VMEM(inverse_self.shape, BF16),
            pltpu.VMEM(coupling.shape, BF16),
            vmem(*sketch.shape),
            vmem(blocks, (slots + 1) * r, rows),
            vmem(g_size, 8 * r, rows),
            vmem(g_size, 2 * r, rows),
            vmem(g_size, 2 * r, rows),
            vmem(2, 2 * r, rows),
            vmem(r // 2, 2 * blocks * r),
            vmem(2, r // 2, 2 * blocks * r),
            vmem(g_size, 2 * r, wide),
            vmem(g_size, blocks * wide, rows),
            vmem(others, blocks * wide, rows),
            pltpu.SMEM(neighbour_mask.shape, neighbour_mask.dtype),
            dma(2 + 2 * blocks + blocks * slots),
            dma(6),
            dma(6),
            dma(8, others),
            dma(8, others),
            dma(blocks, others),
            dma(blocks, others),
            dma(2, blocks),
            dma(2, blocks),
            dma(blocks, others),
            dma(blocks, others),
            dma(blocks, others),
            dma(blocks, others),
            dma(2),
            dma(2),
            dma(others),
            dma(others),
        ],
        compiler_params=pltpu.CompilerParams(
            collective_id=0, has_side_effects=True, vmem_limit_bytes=60 * 1024 * 1024
        ),
        cost_estimate=pl.CostEstimate(
            flops=flops, bytes_accessed=2 * (coupling.size + inverse_self.size), transcendentals=0
        ),
        name="basis_currents",
    )(excitation, inverse_self, coupling, neighbour_mask, sketch)
    return jnp.swapaxes(bases, 1, 2), reduced, driven


def solution(mesh):
    return jax.shard_map(
        functools.partial(shards, mesh.shape["grp"], mesh.shape["blk"]),
        mesh=mesh,
        in_specs=(
            P("blk", None, None),
            P("blk", "grp", None),
            P("blk", None, "grp", None),
            P("blk", None),
            P(),
        ),
        out_specs=(P("blk", "grp", None), P("blk", None, None, None), P("blk", None, None)),
        check_vma=False,
    )
```
